32 devices in a mesh: segment: 2 (over core), seq: 16 (over z, y, x).
Axes of the slice: x: 2, y: 2, z: 4, core: 2. Of those that a mesh axis runs over, the one named last changes fastest.
Arguments:
- tracks_in: bfloat16 [1, 16, 512, 1536], P(None, 'seq'), may hold values from -120 to 120
- w_qkv: bfloat16 [2, 1536, 2304], P('segment'), may hold values from -0.15625 to 0.15625
- w_out: bfloat16 [2, 768, 1536], P('segment'), may hold values from -0.21875 to 0.21875
- visible: int32 [1, 16, 512], P(None, 'seq'), may hold values 0 or 1
- neighbours: int32 [1, 1, 4, 2], replicated, may hold values from 0 to 3, as said below
Outputs:
- section_tokens: bfloat16 [2, 1, 16, 512, 1536], P('segment', None, 'seq')
The draws below stay inside these ranges and needn't reach their ends.
Inputs may be any that keep to these rules, and one draw needn't show every extreme that they name: `neighbours`: each row names 2 different track blocks, none of them the row's own block.
All inputs are finite; a program needn't handle non-finite values. No bound on the sum of `visible` on one device may be relied on, other than what follows from the above.
Results may differ from the reference program's by a relative error of at most 0.0042.
Values may be sent and summed in bfloat16 or wider, within the bound.
A program may use at most 128 MiB of HBM per device.

```python
import math
import jax
import jax.numpy as jnp
from jax import lax

D = 1536
HEADS = 6
HDIM = 128
TRACKS = 512
BLOCK = 128
NB = 2
FRAMES = 16
MB = 1
VIDEOS = 1
GROUPS = 16
TRACK_DEV = 32
BLOCKS = 4
N_SEQ = 16


def draw_tracks_in(key, part):
    subkeys = jax.random.split(key, 3)
    feature_scale = jnp.exp(jax.random.uniform(subkeys[0], (D,), jnp.float32, -1.15, 1.15))
    row_scale = jnp.exp(jax.random.uniform(subkeys[1], (MB, GROUPS, TRACKS, 1), jnp.float32, -1.15, 1.15))
    values_base = jax.random.normal(subkeys[2], (MB, GROUPS, TRACKS, D), jnp.float32)
    return (values_base * row_scale * feature_scale).astype(jnp.bfloat16)


def draw_neighbours(key, part):
    draw_scores = jax.random.randint(key, (MB, VIDEOS, BLOCKS, BLOCKS - 1), 0, 1048576) * (BLOCKS - 1)
    draw_scores = draw_scores + jnp.arange(BLOCKS - 1, dtype=jnp.int32)
    ordering = jnp.argsort(draw_scores, axis=-1, stable=True)[..., :NB].astype(jnp.int32)
    own_block = jnp.arange(BLOCKS, dtype=jnp.int32).reshape(1, 1, BLOCKS, 1)
    return ((own_block + 1 + ordering) % BLOCKS).astype(jnp.int32)


def touch_ends(values, key, least, top_value):
    index_at = [jax.random.randint(jax.random.fold_in(key, axis), (), 0, length) for axis, length in enumerate(values.shape)]
    main_axis = values.shape.index(max(values.shape))
    next_to = index_at[:main_axis] + [(index_at[main_axis] + 1) % values.shape[main_axis]] + index_at[main_axis + 1:]
    return values.at[tuple(index_at)].set(least).at[tuple(next_to)].set(top_value)


def shard_levels(stream_key, shape, cuts, least, high):
    loudness = 1.0
    for dim, blocks in cuts:
        heights = jax.random.uniform(jax.random.fold_in(jax.random.fold_in(stream_key, 6), dim), (blocks,), jnp.float32, least / len(cuts), high / len(cuts))
        loudness = loudness * jnp.repeat(jnp.exp(heights), shape[dim] // blocks).reshape((-1,) + (1,) * (len(shape) - 1 - dim))
    return loudness


def scatter_about(rng, extent, scale, reach, pieces=(), held_as=jnp.bfloat16):
    level = shard_levels(rng, extent, pieces, -0.22, 0.18) if pieces else 1.0
    drawn = jax.random.normal(rng, extent, jnp.float32) * scale * level
    return jnp.minimum(jnp.maximum(drawn, -reach), reach).astype(held_as)


def setup_inputs(seed: int = 0) -> dict:
    arg_keys = jax.random.split(jax.random.key(seed), 6)
    tracks_in = draw_tracks_in(jax.random.fold_in(arg_keys[5], 71), 0)
    w_qkv = scatter_about(arg_keys[1], (2, D, 3 * HEADS * HDIM), D ** -0.5, 0.15625, ((0, 2),))
    w_out = scatter_about(arg_keys[2], (2, HEADS * HDIM, D), (HEADS * HDIM) ** -0.5, 0.21875, ((0, 2),))
    visible = touch_ends((jax.random.randint(arg_keys[3], (MB, GROUPS, TRACKS), 0, 4) < 3).astype(jnp.int32), jax.random.fold_in(arg_keys[3], 1), 0, 1)
    neighbours = draw_neighbours(jax.random.fold_in(arg_keys[5], 71), 0)
    return {"tracks_in": tracks_in, "w_qkv": w_qkv, "w_out": w_out, "visible": visible, "neighbours": neighbours}


epsilon = 1e-06

def normalize(tokens):
    widened = tokens.astype(jnp.float32)
    factor = lax.rsqrt(lax.optimization_barrier(jnp.mean(widened * widened, axis=-1, keepdims=True)) + epsilon)
    return (widened * factor).astype(jnp.bfloat16)

def project(tokens, weight):
    return jnp.dot(normalize(tokens), weight, preferred_element_type=jnp.float32).astype(jnp.bfloat16)

def finish(tokens, mixed_heads, weight):
    delta_rows = jnp.dot(mixed_heads, weight, preferred_element_type=jnp.float32)
    return (tokens.astype(jnp.float32) + delta_rows).astype(jnp.bfloat16)

def time_mix(projected):
    leading = projected.shape[:3]
    shaped = projected.astype(jnp.float32).reshape(leading + (3, HEADS, HDIM))
    queries = shaped[:, :, :, 0]
    keys_all = shaped[:, :, :, 1]
    values = shaped[:, :, :, 2]
    scores = jnp.einsum('vfphd,vgphd->vphfg', queries, keys_all) / math.sqrt(HDIM)
    exponent = jnp.exp(scores)
    weights = (exponent / lax.optimization_barrier(jnp.sum(exponent, axis=-1, keepdims=True))).astype(jnp.bfloat16)
    mixed_heads = jnp.einsum('vphfg,vgphd->vfphd', weights.astype(jnp.float32), values)
    return mixed_heads.reshape(leading + (HEADS * HDIM,)).astype(jnp.bfloat16)

def track_mix(projected, seen_mask, chosen):
    blocks_all = projected.astype(jnp.float32).reshape(BLOCKS, BLOCK, 3, HEADS, HDIM)
    own_block = lax.broadcasted_iota(jnp.int32, (BLOCKS, 1), 0)
    listing = jnp.concatenate([own_block, chosen.astype(jnp.int32)], axis=1)
    queries = blocks_all[:, :, 0]
    keys_sel = jnp.take(blocks_all[:, :, 1], listing, axis=0)
    values_sel = jnp.take(blocks_all[:, :, 2], listing, axis=0)
    seen_sel = jnp.take(seen_mask.reshape(BLOCKS, BLOCK), listing, axis=0)
    scores = jnp.einsum('bqhd,bjkhd->bhqjk', queries, keys_sel) / math.sqrt(HDIM)
    itself = (lax.broadcasted_iota(jnp.int32, (BLOCK, NB + 1, BLOCK), 1) == 0) & (lax.broadcasted_iota(jnp.int32, (BLOCK, NB + 1, BLOCK), 0) == lax.broadcasted_iota(jnp.int32, (BLOCK, NB + 1, BLOCK), 2))
    allowed = (seen_sel[:, None, None, :, :] == 1) | itself[None, None]
    exponent = jnp.where(allowed, jnp.exp(scores), jnp.zeros_like(scores))
    totals = lax.optimization_barrier(jnp.sum(exponent, axis=(-2, -1), keepdims=True))
    weights = (exponent / totals).astype(jnp.bfloat16)
    mixed_heads = jnp.einsum('bhqjk,bjkhd->bqhd', weights.astype(jnp.float32), values_sel)
    return mixed_heads.reshape(TRACKS, HEADS * HDIM).astype(jnp.bfloat16)

def reference(tracks_in, w_qkv, w_out, visible, neighbours):

    def one_batch(entries):
        tokens, seen_all, lists = entries
        flat_in = tokens.reshape(GROUPS * TRACKS, D)
        proj_first = project(flat_in, w_qkv[0]).reshape(VIDEOS, FRAMES, TRACKS, 3 * HEADS * HDIM)
        mixed_first = time_mix(proj_first).reshape(GROUPS * TRACKS, HEADS * HDIM)
        first = finish(flat_in, mixed_first, w_out[0])
        proj_second = project(first, w_qkv[1]).reshape(GROUPS, TRACKS, 3 * HEADS * HDIM)
        group_lists = jnp.repeat(lists, FRAMES, axis=0)
        mixed_second = lax.map(lambda parts: track_mix(parts[0], parts[1], parts[2]), (proj_second, seen_all, group_lists))
        second = finish(first, mixed_second.reshape(GROUPS * TRACKS, HEADS * HDIM), w_out[1])
        regrouped = first.reshape(GROUPS, N_SEQ, TRACK_DEV, D).transpose(1, 0, 2, 3).reshape(N_SEQ, GROUPS * TRACK_DEV, D)
        return (regrouped, second.reshape(GROUPS, TRACKS, D))
    firsts, seconds = lax.map(one_batch, (tracks_in, visible, neighbours))
    return jnp.stack([firsts, seconds])
```

```python
import functools
import math

import jax
import jax.numpy as jnp
from jax import lax
from jax.experimental import pallas as pl
from jax.experimental.pallas import tpu as pltpu
from jax.sharding import PartitionSpec as P

HEADS = 6
HDIM = 128
BLOCK = 128
NB = 2
FRAMES = 16


epsilon = 1e-06


def partner(shard, axis, distance):
    return lax.ppermute(shard, axis, [(i, i ^ 1 << distance) for i in range(lax.axis_size(axis))])


def from_behind(value, axis, steps):
    count = lax.axis_size(axis)
    initial, last = (max(0, -steps), min(count, count - steps))
    return lax.ppermute(value, axis, [(source, source + steps) for source in range(initial, last)])


def normalize(tokens):
    widened = tokens.astype(jnp.float32)
    factor = lax.rsqrt(jnp.mean(widened * widened, axis=-1, keepdims=True) + epsilon)
    return (widened * factor).astype(jnp.bfloat16)


def project(tokens, weight):
    return jnp.dot(normalize(tokens), weight, preferred_element_type=jnp.float32).astype(
        jnp.bfloat16
    )


def finish(tokens, mixed_heads, weight):
    delta_rows = jnp.dot(mixed_heads, weight, preferred_element_type=jnp.float32)
    return (tokens.astype(jnp.float32) + delta_rows).astype(jnp.bfloat16)


def time_branch(projected, count, seq_size):
    inner = HEADS * HDIM
    shaped = projected.reshape(seq_size // FRAMES, FRAMES, count, 3, HEADS, HDIM)
    scores = jnp.einsum(
        "vfphd,vgphd->vphfg",
        shaped[:, :, :, 0],
        shaped[:, :, :, 1],
        preferred_element_type=jnp.float32,
    ) / math.sqrt(HDIM)
    exponent = jnp.exp(scores)
    weights = (exponent / jnp.sum(exponent, axis=-1, keepdims=True)).astype(jnp.bfloat16)
    mixed_heads = jnp.einsum(
        "vphfg,vgphd->vfphd", weights, shaped[:, :, :, 2], preferred_element_type=jnp.float32
    )
    return mixed_heads.reshape(-1, inner).astype(jnp.bfloat16)


def track_branch(projected, seen_mask, chosen, start_block, count):
    inner = HEADS * HDIM
    blocks_count = projected.shape[0] // BLOCK
    blocks_all = projected.reshape(blocks_count, BLOCK, 3, HEADS, HDIM)
    own_block = lax.broadcasted_iota(jnp.int32, (count, 1), 0) + start_block
    listing = jnp.concatenate(
        [own_block, lax.dynamic_slice_in_dim(chosen, start_block, count, 0)], axis=1
    )
    queries = lax.dynamic_slice_in_dim(blocks_all[:, :, 0], start_block, count, 0)
    keys_sel = jnp.take(blocks_all[:, :, 1], listing, axis=0)
    values_sel = jnp.take(blocks_all[:, :, 2], listing, axis=0)
    seen_sel = jnp.take(seen_mask.reshape(blocks_count, BLOCK), listing, axis=0)
    scores = jnp.einsum(
        "bqhd,bjkhd->bhqjk", queries, keys_sel, preferred_element_type=jnp.float32
    ) / math.sqrt(HDIM)
    shape_mask = (BLOCK, NB + 1, BLOCK)
    itself = (lax.broadcasted_iota(jnp.int32, shape_mask, 1) == 0) & (
        lax.broadcasted_iota(jnp.int32, shape_mask, 0)
        == lax.broadcasted_iota(jnp.int32, shape_mask, 2)
    )
    allowed = (seen_sel[:, None, None, :, :] == 1) | itself[None, None]
    exponent = jnp.where(allowed, jnp.exp(scores), jnp.zeros_like(scores))
    totals = jnp.sum(exponent, axis=(-2, -1), keepdims=True)
    weights = (exponent / totals).astype(jnp.bfloat16)
    mixed_heads = jnp.einsum(
        "bhqjk,bjkhd->bqhd", weights, values_sel, preferred_element_type=jnp.float32
    )
    return mixed_heads.reshape(count * BLOCK, inner).astype(jnp.bfloat16)


def on_device(tracks_in, w_qkv, w_out, visible, neighbours):
    segment_no = lax.axis_index("segment")
    seq_no = lax.axis_index("seq")
    seq_size = lax.axis_size("seq")
    segment_size = lax.axis_size("segment")
    tracks = tracks_in.shape[2]
    width = tracks_in.shape[3]
    per_device = tracks // seq_size
    blocks_count = tracks // BLOCK
    video_no = seq_no // FRAMES
    w_both, out_both = (
        lax.all_gather(w_qkv, "segment", axis=0, tiled=True),
        lax.all_gather(w_out, "segment", axis=0, tiled=True),
    )
    half = per_device // segment_size
    query_blocks = blocks_count // segment_size
    start_block = segment_no * query_blocks
    pieces = tracks_in[0, 0].reshape(seq_size, per_device, width)
    mine = lax.dynamic_slice_in_dim(pieces, segment_no * half, half, 1)
    moved = lax.all_to_all(mine, "seq", split_axis=0, concat_axis=0, tiled=True)
    flat = moved.reshape(seq_size * half, width)
    mixed_time = time_branch(project(flat, w_both[0]), half, seq_size)
    first_half = finish(flat, mixed_time, out_both[0]).reshape(seq_size, half, width)
    other_half = partner(first_half, "segment", 0)
    full_first = jnp.where(
        segment_no == 0,
        jnp.concatenate([first_half, other_half], axis=1),
        jnp.concatenate([other_half, first_half], axis=1),
    )
    frame_rows = lax.all_to_all(full_first, "seq", split_axis=0, concat_axis=0, tiled=True).reshape(
        tracks, width
    )
    projected = project(frame_rows, w_both[1])
    lists_now = lax.dynamic_index_in_dim(neighbours[0], video_no, 0, keepdims=False)
    mixed_track = track_branch(projected, visible[0, 0], lists_now, start_block, query_blocks)
    own_rows = lax.dynamic_slice_in_dim(frame_rows, start_block * BLOCK, query_blocks * BLOCK, 0)
    second_part = finish(own_rows, mixed_track, out_both[1])
    lower_part = from_behind(second_part, "segment", 1)
    full_second = jnp.concatenate([lower_part, second_part], axis=0)
    finals = [jnp.where(segment_no == 0, full_first.reshape(tracks, width), full_second)]
    return jnp.stack(finals)[None, :, None]


INNER = HEADS * HDIM
HALF_HEADS = HEADS // 2
HALF_INNER = HALF_HEADS * HDIM
MESH = pl.DeviceIdType.MESH
SCALE_LOG2 = math.log2(math.e) / math.sqrt(HDIM)


def dot(a, b):
    return jnp.dot(a, b, preferred_element_type=jnp.float32)


def dot_t(a, b):
    return lax.dot_general(a, b, (((1,), (1,)), ((), ())), preferred_element_type=jnp.float32)


def fused_kernel(
    n,
    half,
    x_ref,
    wq_ref,
    wo_ref,
    seen_ref,
    near_ref,
    out_ref,
    wq0,
    wo0,
    wq1,
    wo1,
    x_got,
    x_norm,
    x_frame,
    qkv0,
    mix0,
    first0,
    mix_frame,
    first1,
    qkv1,
    mix1,
    mix1_low,
    second,
    w_sem,
    w_send,
    x_send,
    x_recv,
    frame_sem,
    m_send,
    m_recv,
    f_send,
    f_recv,
    low_send,
    low_recv,
    out_sem,
    out_send,
    out_recv,
):
    s = lax.axis_index("segment")
    me = lax.axis_index("seq")
    sibling = {"segment": 1 - s, "seq": me}
    group = 2 * half
    tokens = n * half
    tracks = n * group
    blocks = tracks // BLOCK

    def peer(d):
        return {"segment": s, "seq": d}

    barrier = pltpu.get_barrier_semaphore()

    def greet(k, c):
        pl.semaphore_signal(
            barrier, inc=1, device_id=peer(lax.rem(me + k, n)), device_id_type=MESH
        )
        return c

    lax.fori_loop(1, n, greet, 0)
    pl.semaphore_signal(barrier, inc=1, device_id=sibling, device_id_type=MESH)

    def rows(index, size):
        return pl.ds(pl.multiple_of(index * size, size), size)

    def x_copy(d, source):
        return pltpu.make_async_remote_copy(
            src_ref=x_ref.at[rows(2 * d + s, half), :],
            dst_ref=x_got.at[rows(source, half), :],
            send_sem=x_send.at[d],
            recv_sem=x_recv.at[source],
            device_id=peer(d),
            device_id_type=MESH,
        )

    def wq1_cols(core, j):
        return pl.ds(pl.multiple_of(j * INNER + core * HALF_INNER, HDIM), HALF_INNER)

    def wq1_dst(j):
        return wq1.at[:, pl.ds(j * HALF_INNER, HALF_INNER)]

    own_x = pltpu.make_async_copy(
        x_ref.at[rows(2 * me + s, half), :], x_got.at[rows(me, half), :], x_recv.at[me]
    )
    frame_copy = pltpu.make_async_copy(x_ref, x_frame, frame_sem)
    wq0_local = pltpu.make_async_copy(wq_ref, wq0, w_sem.at[0])
    wo0_local = pltpu.make_async_copy(wo_ref, wo0, w_sem.at[1])
    wo1_local = pltpu.make_async_copy(wo_ref, wo1, w_sem.at[2])
    wq1_local = [
        pltpu.make_async_copy(wq_ref.at[:, wq1_cols(s, j)], wq1_dst(j), w_sem.at[3 + j])
        for j in range(3)
    ]
    wq0_remote = pltpu.make_async_remote_copy(
        wq_ref, wq0, w_send.at[0], w_sem.at[0], device_id=sibling, device_id_type=MESH
    )
    wo0_remote = pltpu.make_async_remote_copy(
        wo_ref, wo0, w_send.at[1], w_sem.at[1], device_id=sibling, device_id_type=MESH
    )
    wq1_remote = [
        pltpu.make_async_remote_copy(
            wq_ref.at[:, wq1_cols(1 - s, j)],
            wq1_dst(j),
            w_send.at[2 + j],
            w_sem.at[3 + j],
            device_id=sibling,
            device_id_type=MESH,
        )
        for j in range(3)
    ]

    pl.semaphore_wait(barrier, n)

    def send_x(k, c):
        x_copy(lax.rem(me + k, n), me).start()
        return c

    lax.fori_loop(1, n, send_x, 0)

    @pl.when(s == 0)
    def _():
        wq0_remote.start()
        wo0_remote.start()

    own_x.start()

    @pl.when(s == 0)
    def _():
        wq0_local.start()
        wo0_local.start()

    @pl.when(s == 1)
    def _():
        for copy in wq1_remote + wq1_local:
            copy.start()
        wo1_local.start()

    frame_copy.start()

    def norm_rows(k, c):
        source = lax.rem(me + n - k, n)

        @pl.when(k > 0)
        def _():
            x_copy(source, source).wait_recv()

        @pl.when(k == 0)
        def _():
            own_x.wait()

        x_norm[rows(source, half), :] = normalize(x_got[rows(source, half), :])
        return c

    lax.fori_loop(0, n, norm_rows, 0)

    @pl.when(s == 0)
    def _():
        wq0_local.wait()

    @pl.when(s == 1)
    def _():
        wq0_remote.wait_recv()

    def project0(j, c):
        columns = rows(j, 768)
        qkv0[:, columns] = dot(x_norm[...], wq0[:, columns]).astype(jnp.bfloat16)
        return c

    lax.fori_loop(0, 3 * INNER // 768, project0, 0)

    i0 = lax.broadcasted_iota(jnp.int32, (tokens, tokens), 0)
    i1 = lax.broadcasted_iota(jnp.int32, (tokens, tokens), 1)
    same = lax.rem(i0, half) == lax.rem(i1, half)
    for h in range(HEADS):
        q = qkv0[:, h * HDIM : (h + 1) * HDIM]
        k = qkv0[:, INNER + h * HDIM : INNER + (h + 1) * HDIM]
        v = qkv0[:, 2 * INNER + h * HDIM : 2 * INNER + (h + 1) * HDIM]
        e = jnp.where(same, jnp.exp2(dot_t(q, k) * SCALE_LOG2), 0.0)
        w = (e * (1.0 / jnp.sum(e, axis=-1, keepdims=True))).astype(jnp.bfloat16)
        mix0[:, h * HDIM : (h + 1) * HDIM] = dot(w, v).astype(jnp.bfloat16)

    def m_copy(f, source):
        return pltpu.make_async_remote_copy(
            src_ref=mix0.at[rows(f, half), :],
            dst_ref=mix_frame.at[rows(2 * source + s, half), :],
            send_sem=m_send.at[f],
            recv_sem=m_recv.at[source],
            device_id=peer(f),
            device_id_type=MESH,
        )

    def f_copy(d, core):
        return pltpu.make_async_remote_copy(
            src_ref=mix_frame.at[rows(2 * d + core, half), :],
            dst_ref=mix_frame.at[rows(2 * d + core, half), :],
            send_sem=f_send.at[d],
            recv_sem=f_recv.at[d],
            device_id=sibling,
            device_id_type=MESH,
        )

    def send_m(k, c):
        m_copy(lax.rem(me + k, n), me).start()
        return c

    lax.fori_loop(1, n, send_m, 0)
    mix_frame[rows(2 * me + s, half), :] = mix0[rows(me, half), :]
    f_copy(me, s).start()

    @pl.when(s == 0)
    def _():
        wo0_local.wait()

    @pl.when(s == 1)
    def _():
        wo0_remote.wait_recv()

    added = x_got[...].astype(jnp.float32) + dot(mix0[...], wo0[...])
    first0[...] = added.astype(jnp.bfloat16).reshape(n, half, -1)
    out_first = pltpu.make_async_copy(first0, out_ref.at[:, 0], out_sem.at[0])
    out_remote = pltpu.make_async_remote_copy(
        first0, out_ref.at[:, 1], out_send, out_recv, device_id=sibling, device_id_type=MESH
    )

    @pl.when(s == 0)
    def _():
        out_first.start()

    @pl.when(s == 1)
    def _():
        out_remote.start()

    frame_copy.wait()

    def forward(k, c):
        source = lax.rem(me + n - k, n)
        m_copy(source, source).wait_recv()
        f_copy(source, s).start()
        return c

    lax.fori_loop(1, n, forward, 0)

    def forwarded(k, c):
        f_copy(lax.rem(me + n - k, n), 1 - s).wait_recv()
        return c

    lax.fori_loop(0, n, forwarded, 0)
    for j in range(3):

        @pl.when(s == 0)
        def _():
            wq1_remote[j].wait_recv()

        @pl.when(s == 1)
        def _():
            wq1_local[j].wait()

    def middle(i, c):
        part = rows(i, 256)
        grown = x_frame[part, :].astype(jnp.float32) + dot(mix_frame[part, :], wo0[...])
        grown = grown.astype(jnp.bfloat16)
        first1[part, :] = grown
        qkv1[part, :] = dot(normalize(grown), wq1[...]).astype(jnp.bfloat16)
        return c

    lax.fori_loop(0, tracks // 256, middle, 0)

    r = lax.broadcasted_iota(jnp.int32, (BLOCK, tracks), 0)
    t = lax.broadcasted_iota(jnp.int32, (BLOCK, tracks), 1)
    track = lax.broadcasted_iota(jnp.int32, (1, tracks), 1)
    block_of = track // BLOCK
    seen = seen_ref[...] == 1

    def low_copy(b):
        return pltpu.make_async_remote_copy(
            src_ref=mix1.at[rows(b, BLOCK), :],
            dst_ref=mix1_low.at[rows(b, BLOCK), :],
            send_sem=low_send.at[b],
            recv_sem=low_recv.at[b],
            device_id=sibling,
            device_id_type=MESH,
        )

    def attend(b, c):
        part = rows(b, BLOCK)
        listed = (block_of == b) | (block_of == near_ref[b, 0]) | (block_of == near_ref[b, 1])
        open_row = jnp.where(seen & listed, 1.0, 0.0)
        allow = jnp.where(t == r + b * BLOCK, 1.0, open_row) > 0.5
        for h in range(HALF_HEADS):
            q = qkv1[part, h * HDIM : (h + 1) * HDIM]
            k = qkv1[:, HALF_INNER + h * HDIM : HALF_INNER + (h + 1) * HDIM]
            v = qkv1[:, 2 * HALF_INNER + h * HDIM : 2 * HALF_INNER + (h + 1) * HDIM]
            e = jnp.where(allow, jnp.exp2(dot_t(q, k) * SCALE_LOG2), 0.0)
            w = (e * (1.0 / jnp.sum(e, axis=-1, keepdims=True))).astype(jnp.bfloat16)
            mix1[part, h * HDIM : (h + 1) * HDIM] = dot(w, v).astype(jnp.bfloat16)

        @pl.when(s == 0)
        def _():
            low_copy(b).start()

        return c

    lax.fori_loop(0, blocks, attend, 0)
    per_block = BLOCK // group

    def out_copy(b):
        return pltpu.make_async_copy(
            second.at[rows(b, per_block)], out_ref.at[rows(b, per_block)], out_sem.at[1 + b]
        )

    @pl.when(s == 1)
    def _():
        wo1_local.wait()

        def close(b, c):
            part = rows(b, BLOCK)
            low_copy(b).wait_recv()
            delta = dot(mix1_low[part, :], wo1[:HALF_INNER, :]) + dot(
                mix1[part, :], wo1[HALF_INNER:, :]
            )
            total = (first1[part, :].astype(jnp.float32) + delta).astype(jnp.bfloat16)
            second[rows(b, per_block)] = total.reshape(per_block, 2, half, -1)
            out_copy(b).start()
            return c

        lax.fori_loop(0, blocks, close, 0)

        def closed(b, c):
            out_copy(b).wait()
            return c

        lax.fori_loop(0, blocks, closed, 0)
        out_remote.wait_send()
        for copy in wq1_remote:
            copy.wait_send()

    @pl.when(s == 0)
    def _():
        out_first.wait()
        out_remote.wait_recv()
        wq0_remote.wait_send()
        wo0_remote.wait_send()

        def sent_low(b, c):
            low_copy(b).wait_send()
            return c

        lax.fori_loop(0, blocks, sent_low, 0)

    def drain(k, c):
        d = lax.rem(me + k, n)
        x_copy(d, me).wait_send()
        m_copy(d, me).wait_send()
        f_copy(d, s).wait_send()
        return c

    lax.fori_loop(1, n, drain, 0)
    f_copy(me, s).wait_send()


def on_device_fused(tracks_in, w_qkv, w_out, visible, neighbours):
    n = lax.axis_size("seq")
    tracks, width = tracks_in.shape[2:]
    half = tracks // n // 2
    tokens = n * half
    blocks = tracks // BLOCK
    bf16 = jnp.bfloat16
    dma = pltpu.SemaphoreType.DMA
    anywhere = pl.BlockSpec(memory_space=pl.ANY)
    out = pl.pallas_call(
        functools.partial(fused_kernel, n, half),
        out_shape=jax.ShapeDtypeStruct((n, 2, half, width), bf16),
        in_specs=[anywhere] * 3
        + [pl.BlockSpec(memory_space=pltpu.VMEM), pl.BlockSpec(memory_space=pltpu.SMEM)],
        out_specs=anywhere,
        scratch_shapes=[
            pltpu.VMEM((width, 3 * INNER), bf16),
            pltpu.VMEM((INNER, width), bf16),
            pltpu.VMEM((width, 3 * HALF_INNER), bf16),
            pltpu.VMEM((INNER, width), bf16),
            pltpu.VMEM((tokens, width), bf16),
            pltpu.VMEM((tokens, width), bf16),
            pltpu.VMEM((tracks, width), bf16),
            pltpu.VMEM((tokens, 3 * INNER), bf16),
            pltpu.VMEM((tokens, INNER), bf16),
            pltpu.VMEM((n, half, width), bf16),
            pltpu.VMEM((tracks, INNER), bf16),
            pltpu.VMEM((tracks, width), bf16),
            pltpu.VMEM((tracks, 3 * HALF_INNER), bf16),
            pltpu.VMEM((tracks, HALF_INNER), bf16),
            pltpu.VMEM((tracks, HALF_INNER), bf16),
            pltpu.VMEM((n, 2, half, width), bf16),
            dma((6,)),
            dma((5,)),
            dma((n,)),
            dma((n,)),
            dma,
            dma((n,)),
            dma((n,)),
            dma((n,)),
            dma((n,)),
            dma((blocks,)),
            dma((blocks,)),
            dma((1 + blocks,)),
            dma,
            dma,
        ],
        compiler_params=pltpu.CompilerParams(
            collective_id=0, has_side_effects=True, vmem_limit_bytes=56 * 1024 * 1024
        ),
        cost_estimate=pl.CostEstimate(
            flops=9_000_000_000, bytes_accessed=20_000_000, transcendentals=1_200_000
        ),
    )(
        tracks_in.reshape(tracks, width),
        w_qkv.reshape(width, 3 * INNER),
        w_out.reshape(INNER, width),
        visible.reshape(1, tracks),
        neighbours.reshape(blocks, NB),
    )
    return out.reshape(1, 1, 1, tracks, width)


def fits_fused(mesh):
    return mesh.shape["seq"] == FRAMES and mesh.shape["segment"] == 2


def solution(mesh):
    body = on_device_fused if fits_fused(mesh) else on_device
    return jax.shard_map(
        body,
        mesh=mesh,
        in_specs=(
            P(None, "seq", None, None),
            P("segment", None, None),
            P("segment", None, None),
            P(None, "seq", None),
            P(),
        ),
        out_specs=P("segment", None, "seq", None, None),
        check_vma=False,
    )
```

```python
import functools
import math

import jax
import jax.numpy as jnp
from jax import lax
from jax.experimental import pallas as pl
from jax.experimental.pallas import tpu as pltpu
from jax.sharding import PartitionSpec as P

HEADS = 6
HDIM = 128
BLOCK = 128
NB = 2
FRAMES = 16


epsilon = 1e-06


def partner(shard, axis, distance):
    return lax.ppermute(shard, axis, [(i, i ^ 1 << distance) for i in range(lax.axis_size(axis))])


def from_behind(value, axis, steps):
    count = lax.axis_size(axis)
    initial, last = (max(0, -steps), min(count, count - steps))
    return lax.ppermute(value, axis, [(source, source + steps) for source in range(initial, last)])


def normalize(tokens):
    widened = tokens.astype(jnp.float32)
    factor = lax.rsqrt(jnp.mean(widened * widened, axis=-1, keepdims=True) + epsilon)
    return (widened * factor).astype(jnp.bfloat16)


def project(tokens, weight):
    return jnp.dot(normalize(tokens), weight, preferred_element_type=jnp.float32).astype(
        jnp.bfloat16
    )


def finish(tokens, mixed_heads, weight):
    delta_rows = jnp.dot(mixed_heads, weight, preferred_element_type=jnp.float32)
    return (tokens.astype(jnp.float32) + delta_rows).astype(jnp.bfloat16)


def time_branch(projected, count, seq_size):
    inner = HEADS * HDIM
    shaped = projected.reshape(seq_size // FRAMES, FRAMES, count, 3, HEADS, HDIM)
    scores = jnp.einsum(
        "vfphd,vgphd->vphfg",
        shaped[:, :, :, 0],
        shaped[:, :, :, 1],
        preferred_element_type=jnp.float32,
    ) / math.sqrt(HDIM)
    exponent = jnp.exp(scores)
    weights = (exponent / jnp.sum(exponent, axis=-1, keepdims=True)).astype(jnp.bfloat16)
    mixed_heads = jnp.einsum(
        "vphfg,vgphd->vfphd", weights, shaped[:, :, :, 2], preferred_element_type=jnp.float32
    )
    return mixed_heads.reshape(-1, inner).astype(jnp.bfloat16)


def track_branch(projected, seen_mask, chosen, start_block, count):
    inner = HEADS * HDIM
    blocks_count = projected.shape[0] // BLOCK
    blocks_all = projected.reshape(blocks_count, BLOCK, 3, HEADS, HDIM)
    own_block = lax.broadcasted_iota(jnp.int32, (count, 1), 0) + start_block
    listing = jnp.concatenate(
        [own_block, lax.dynamic_slice_in_dim(chosen, start_block, count, 0)], axis=1
    )
    queries = lax.dynamic_slice_in_dim(blocks_all[:, :, 0], start_block, count, 0)
    keys_sel = jnp.take(blocks_all[:, :, 1], listing, axis=0)
    values_sel = jnp.take(blocks_all[:, :, 2], listing, axis=0)
    seen_sel = jnp.take(seen_mask.reshape(blocks_count, BLOCK), listing, axis=0)
    scores = jnp.einsum(
        "bqhd,bjkhd->bhqjk", queries, keys_sel, preferred_element_type=jnp.float32
    ) / math.sqrt(HDIM)
    shape_mask = (BLOCK, NB + 1, BLOCK)
    itself = (lax.broadcasted_iota(jnp.int32, shape_mask, 1) == 0) & (
        lax.broadcasted_iota(jnp.int32, shape_mask, 0)
        == lax.broadcasted_iota(jnp.int32, shape_mask, 2)
    )
    allowed = (seen_sel[:, None, None, :, :] == 1) | itself[None, None]
    exponent = jnp.where(allowed, jnp.exp(scores), jnp.zeros_like(scores))
    totals = jnp.sum(exponent, axis=(-2, -1), keepdims=True)
    weights = (exponent / totals).astype(jnp.bfloat16)
    mixed_heads = jnp.einsum(
        "bhqjk,bjkhd->bqhd", weights, values_sel, preferred_element_type=jnp.float32
    )
    return mixed_heads.reshape(count * BLOCK, inner).astype(jnp.bfloat16)


def on_device(tracks_in, w_qkv, w_out, visible, neighbours):
    segment_no = lax.axis_index("segment")
    seq_no = lax.axis_index("seq")
    seq_size = lax.axis_size("seq")
    segment_size = lax.axis_size("segment")
    tracks = tracks_in.shape[2]
    width = tracks_in.shape[3]
    per_device = tracks // seq_size
    blocks_count = tracks // BLOCK
    video_no = seq_no // FRAMES
    w_both, out_both = (
        lax.all_gather(w_qkv, "segment", axis=0, tiled=True),
        lax.all_gather(w_out, "segment", axis=0, tiled=True),
    )
    half = per_device // segment_size
    query_blocks = blocks_count // segment_size
    start_block = segment_no * query_blocks
    pieces = tracks_in[0, 0].reshape(seq_size, per_device, width)
    mine = lax.dynamic_slice_in_dim(pieces, segment_no * half, half, 1)
    moved = lax.all_to_all(mine, "seq", split_axis=0, concat_axis=0, tiled=True)
    flat = moved.reshape(seq_size * half, width)
    mixed_time = time_branch(project(flat, w_both[0]), half, seq_size)
    first_half = finish(flat, mixed_time, out_both[0]).reshape(seq_size, half, width)
    other_half = partner(first_half, "segment", 0)
    full_first = jnp.where(
        segment_no == 0,
        jnp.concatenate([first_half, other_half], axis=1),
        jnp.concatenate([other_half, first_half], axis=1),
    )
    frame_rows = lax.all_to_all(full_first, "seq", split_axis=0, concat_axis=0, tiled=True).reshape(
        tracks, width
    )
    projected = project(frame_rows, w_both[1])
    lists_now = lax.dynamic_index_in_dim(neighbours[0], video_no, 0, keepdims=False)
    mixed_track = track_branch(projected, visible[0, 0], lists_now, start_block, query_blocks)
    own_rows = lax.dynamic_slice_in_dim(frame_rows, start_block * BLOCK, query_blocks * BLOCK, 0)
    second_part = finish(own_rows, mixed_track, out_both[1])
    lower_part = from_behind(second_part, "segment", 1)
    full_second = jnp.concatenate([lower_part, second_part], axis=0)
    finals = [jnp.where(segment_no == 0, full_first.reshape(tracks, width), full_second)]
    return jnp.stack(finals)[None, :, None]


INNER = HEADS * HDIM
HALF_HEADS = HEADS // 2
HALF_INNER = HALF_HEADS * HDIM
MESH = pl.DeviceIdType.MESH
SCALE_LOG2 = math.log2(math.e) / math.sqrt(HDIM)


def dot(a, b):
    return jnp.dot(a, b, preferred_element_type=jnp.float32)


def dot_t(a, b):
    return lax.dot_general(a, b, (((1,), (1,)), ((), ())), preferred_element_type=jnp.float32)


def fused_kernel(
    n,
    half,
    x_ref,
    wq_ref,
    wo_ref,
    seen_ref,
    near_ref,
    out_ref,
    wq0,
    wo0,
    wq1,
    wo1,
    x_got,
    x_norm,
    x_frame,
    qkv0,
    mix0,
    first0,
    mix_frame,
    first1,
    qkv1,
    mix1,
    mix1_low,
    second,
    wq0_sem,
    wq0_send,
    wq1_sem,
    wq1_send,
    wo_sem,
    wo_send,
    x_send,
    x_recv,
    xf_send,
    xf_recv,
    frame_sem,
    m_send,
    m_recv,
    f_send,
    f_recv,
    up_send,
    up_recv,
    low_send,
    low_recv,
    out_sem,
):
    s = lax.axis_index("segment")
    me = lax.axis_index("seq")
    sibling = {"segment": 1 - s, "seq": me}
    group = 2 * half
    tokens = n * half
    tracks = n * group
    blocks = tracks // BLOCK

    def peer(d):
        return {"segment": s, "seq": d}

    barrier = pltpu.get_barrier_semaphore()

    def greet(k, c):
        pl.semaphore_signal(
            barrier, inc=1, device_id=peer(lax.rem(me + k, n)), device_id_type=MESH
        )
        return c

    lax.fori_loop(1, n, greet, 0)
    pl.semaphore_signal(barrier, inc=1, device_id=sibling, device_id_type=MESH)

    def rows(index, size):
        return pl.ds(pl.multiple_of(index * size, size), size)

    def local(src, dst, sem):
        return pltpu.make_async_copy(src, dst, sem)

    def remote(src, dst, send, recv, device):
        return pltpu.make_async_remote_copy(
            src_ref=src,
            dst_ref=dst,
            send_sem=send,
            recv_sem=recv,
            device_id=device,
            device_id_type=MESH,
        )

    def x_copy(d, source):
        return remote(
            x_ref.at[rows(2 * d + s, half), :],
            x_got.at[rows(s * n + source, half), :],
            x_send.at[d],
            x_recv.at[source],
            peer(d),
        )

    def xf_copy(source, core):
        place = rows(core * n + source, half)
        return remote(
            x_got.at[place, :], x_got.at[place, :], xf_send.at[source], xf_recv.at[source], sibling
        )

    def head_cols(core, j):
        return pl.ds(pl.multiple_of(j * INNER + core * HALF_INNER, HDIM), HALF_INNER)

    def packed(w, j):
        return w.at[:, pl.ds(j * HALF_INNER, HALF_INNER)]

    own_x = local(
        x_ref.at[rows(2 * me + s, half), :], x_got.at[rows(s * n + me, half), :], x_recv.at[me]
    )
    frame_copy = local(x_ref, x_frame, frame_sem)
    wq0_local = [
        local(wq_ref.at[:, head_cols(s, j)], packed(wq0, j), wq0_sem.at[j]) for j in range(3)
    ]
    wq1_local = [
        local(wq_ref.at[:, head_cols(s, j)], packed(wq1, j), wq1_sem.at[j]) for j in range(3)
    ]
    wq0_remote = [
        remote(
            wq_ref.at[:, head_cols(1 - s, j)],
            packed(wq0, j),
            wq0_send.at[j],
            wq0_sem.at[j],
            sibling,
        )
        for j in range(3)
    ]
    wq1_remote = [
        remote(
            wq_ref.at[:, head_cols(1 - s, j)],
            packed(wq1, j),
            wq1_send.at[j],
            wq1_sem.at[j],
            sibling,
        )
        for j in range(3)
    ]
    wo0_local = local(wo_ref, wo0, wo_sem.at[0])
    wo1_local = local(wo_ref, wo1, wo_sem.at[1])
    wo0_remote = remote(wo_ref, wo0, wo_send, wo_sem.at[0], sibling)

    pl.semaphore_wait(barrier, n)

    def send_x(k, c):
        x_copy(lax.rem(me + k, n), me).start()
        return c

    lax.fori_loop(1, n, send_x, 0)
    own_x.start()

    @pl.when(s == 0)
    def _():
        for copy in wq0_remote + wq0_local:
            copy.start()
        wo0_remote.start()
        wo0_local.start()

    @pl.when(s == 1)
    def _():
        for copy in wq1_remote + wq1_local:
            copy.start()
        wo1_local.start()

    frame_copy.start()

    def take_x(k, c):
        source = lax.rem(me + n - k, n)

        @pl.when(k > 0)
        def _():
            x_copy(source, source).wait_recv()

        @pl.when(k == 0)
        def _():
            own_x.wait()

        xf_copy(source, s).start()
        place = rows(s * n + source, half)
        x_norm[place, :] = normalize(x_got[place, :])
        return c

    def take_xf(k, c):
        source = lax.rem(me + n - k, n)
        xf_copy(source, 1 - s).wait_recv()
        place = rows((1 - s) * n + source, half)
        x_norm[place, :] = normalize(x_got[place, :])
        return c

    lax.fori_loop(0, n, take_x, 0)
    for j in range(3):

        @pl.when(s == 0)
        def _():
            wq0_local[j].wait()

        @pl.when(s == 1)
        def _():
            wq0_remote[j].wait_recv()

    i0 = lax.broadcasted_iota(jnp.int32, (tokens, tokens), 0)
    i1 = lax.broadcasted_iota(jnp.int32, (tokens, tokens), 1)
    same = lax.rem(i0, half) == lax.rem(i1, half)
    own_cols = pl.ds(pl.multiple_of(s * HALF_INNER, HDIM), HALF_INNER)

    def m_copy(f, source, g):
        return remote(
            mix0.at[rows(g * n + f, half), own_cols],
            mix_frame.at[rows(2 * source + g, half), own_cols],
            m_send.at[g * n + f],
            m_recv.at[g * n + source],
            peer(f),
        )

    def f_copy(d, core, g):
        place = mix_frame.at[
            rows(2 * d + g, half), pl.ds(pl.multiple_of(core * HALF_INNER, HDIM), HALF_INNER)
        ]
        return remote(place, place, f_send.at[g * n + d], f_recv.at[g * n + d], sibling)

    def up_copy(g):
        place = mix0.at[rows(g, tokens), pl.ds(HALF_INNER, HALF_INNER)]
        return remote(place, place, up_send.at[g], up_recv.at[g], sibling)

    def time_half(order, c):
        g = jnp.where(order == 0, s, 1 - s)
        part = rows(g, tokens)

        @pl.when(order == 1)
        def _():
            lax.fori_loop(0, n, take_xf, 0)

        qkv0[...] = dot(x_norm[part, :], wq0[...]).astype(jnp.bfloat16)
        mixed = []
        for h in range(HALF_HEADS):
            q = qkv0[:, h * HDIM : (h + 1) * HDIM]
            k = qkv0[:, HALF_INNER + h * HDIM : HALF_INNER + (h + 1) * HDIM]
            v = qkv0[:, 2 * HALF_INNER + h * HDIM : 2 * HALF_INNER + (h + 1) * HDIM]
            e = jnp.where(same, jnp.exp2(dot_t(q, k) * SCALE_LOG2), 0.0)
            w = (e * (1.0 / jnp.sum(e, axis=-1, keepdims=True))).astype(jnp.bfloat16)
            mixed.append(dot(w, v).astype(jnp.bfloat16))
        mix0[part, own_cols] = jnp.concatenate(mixed, axis=1)

        def send_m(k, c):
            m_copy(lax.rem(me + k, n), me, g).start()
            return c

        lax.fori_loop(1, n, send_m, 0)
        mix_frame[rows(2 * me + g, half), own_cols] = mix0[rows(g * n + me, half), own_cols]
        f_copy(me, s, g).start()

        @pl.when(s == 1)
        def _():
            up_copy(g).start()

        return c

    lax.fori_loop(0, 2, time_half, 0)

    @pl.when(s == 0)
    def _():
        wo0_local.wait()

    @pl.when(s == 1)
    def _():
        wo0_remote.wait_recv()

    def forward(i, c):
        g = jnp.where(i < n - 1, s, 1 - s)
        source = lax.rem(me + n - 1 - lax.rem(i, n - 1), n)
        m_copy(source, source, g).wait_recv()
        f_copy(source, s, g).start()
        return c

    lax.fori_loop(0, n - 1, forward, 0)

    def first_out(g):
        return local(first0.at[g], out_ref.at[:, g], out_sem.at[blocks + g])

    @pl.when(s == 0)
    def _():
        def give(i, c):
            g = 1 - i
            up_copy(g).wait_recv()
            part = rows(g, tokens)
            added = x_got[part, :].astype(jnp.float32) + dot(mix0[part, :], wo0[...])
            first0[g] = added.astype(jnp.bfloat16).reshape(n, half, -1)
            first_out(g).start()
            return c

        lax.fori_loop(0, 2, give, 0)

    lax.fori_loop(n - 1, 2 * (n - 1), forward, 0)
    frame_copy.wait()

    def forwarded(i, c):
        g = jnp.where(i < n, 1 - s, s)
        f_copy(lax.rem(me + n - lax.rem(i, n), n), 1 - s, g).wait_recv()
        return c

    lax.fori_loop(0, 2 * n, forwarded, 0)
    for j in range(3):

        @pl.when(s == 0)
        def _():
            wq1_remote[j].wait_recv()

        @pl.when(s == 1)
        def _():
            wq1_local[j].wait()

    def middle(i, c):
        part = rows(i, 256)
        grown = x_frame[part, :].astype(jnp.float32) + dot(mix_frame[part, :], wo0[...])
        grown = grown.astype(jnp.bfloat16)
        first1[part, :] = grown
        qkv1[part, :] = dot(normalize(grown), wq1[...]).astype(jnp.bfloat16)
        return c

    lax.fori_loop(0, tracks // 256, middle, 0)

    r = lax.broadcasted_iota(jnp.int32, (BLOCK, tracks), 0)
    t = lax.broadcasted_iota(jnp.int32, (BLOCK, tracks), 1)
    block_of = lax.broadcasted_iota(jnp.int32, (1, tracks), 1) // BLOCK
    near_at = lax.broadcasted_iota(jnp.int32, (NB, blocks), 1)
    seen = seen_ref[...] == 1

    def low_copy(b):
        place = rows(b, BLOCK)
        return remote(
            mix1.at[place, :], mix1_low.at[place, :], low_send.at[b], low_recv.at[b], sibling
        )

    def attend(b, c):
        part = rows(b, BLOCK)
        near = jnp.sum(jnp.where(near_at == b, near_ref[...], 0), axis=1, keepdims=True)
        listed = (block_of == b) | (block_of == near[0:1]) | (block_of == near[1:2])
        open_row = jnp.where(seen & listed, 1.0, 0.0)
        allow = jnp.where(t == r + b * BLOCK, 1.0, open_row) > 0.5
        for h in range(HALF_HEADS):
            q = qkv1[part, h * HDIM : (h + 1) * HDIM]
            k = qkv1[:, HALF_INNER + h * HDIM : HALF_INNER + (h + 1) * HDIM]
            v = qkv1[:, 2 * HALF_INNER + h * HDIM : 2 * HALF_INNER + (h + 1) * HDIM]
            e = jnp.where(allow, jnp.exp2(dot_t(q, k) * SCALE_LOG2), 0.0)
            w = (e * (1.0 / jnp.sum(e, axis=-1, keepdims=True))).astype(jnp.bfloat16)
            mix1[part, h * HDIM : (h + 1) * HDIM] = dot(w, v).astype(jnp.bfloat16)

        @pl.when(s == 0)
        def _():
            low_copy(b).start()

        return c

    lax.fori_loop(0, blocks, attend, 0)
    per_block = BLOCK // group

    def out_copy(b):
        return local(second.at[rows(b, per_block)], out_ref.at[rows(b, per_block)], out_sem.at[b])

    @pl.when(s == 1)
    def _():
        wo1_local.wait()

        def close(b, c):
            part = rows(b, BLOCK)
            low_copy(b).wait_recv()
            mixed = jnp.concatenate([mix1_low[part, :], mix1[part, :]], axis=1)
            total = first1[part, :].astype(jnp.float32) + dot(mixed, wo1[...])
            second[rows(b, per_block)] = total.astype(jnp.bfloat16).reshape(
                per_block, 2, half, -1
            )
            out_copy(b).start()
            return c

        lax.fori_loop(0, blocks, close, 0)

        def closed(b, c):
            out_copy(b).wait()
            return c

        lax.fori_loop(0, blocks, closed, 0)
        for copy in wq1_remote:
            copy.wait_send()
        for g in range(2):
            up_copy(g).wait_send()

    @pl.when(s == 0)
    def _():
        for g in range(2):
            first_out(g).wait()
        for copy in wq0_remote + [wo0_remote]:
            copy.wait_send()

        def sent_low(b, c):
            low_copy(b).wait_send()
            return c

        lax.fori_loop(0, blocks, sent_low, 0)

    def drain(k, c):
        d = lax.rem(me + k, n)

        @pl.when(k > 0)
        def _():
            x_copy(d, me).wait_send()
            m_copy(d, me, 0).wait_send()
            m_copy(d, me, 1).wait_send()

        xf_copy(d, s).wait_send()
        f_copy(d, s, 0).wait_send()
        f_copy(d, s, 1).wait_send()
        return c

    lax.fori_loop(0, n, drain, 0)


def on_device_fused(tracks_in, w_qkv, w_out, visible, neighbours):
    n = lax.axis_size("seq")
    tracks, width = tracks_in.shape[2:]
    half = tracks // n // 2
    tokens = n * half
    blocks = tracks // BLOCK
    bf16 = jnp.bfloat16
    dma = pltpu.SemaphoreType.DMA
    anywhere = pl.BlockSpec(memory_space=pl.ANY)
    in_vmem = pl.BlockSpec(memory_space=pltpu.VMEM)
    out = pl.pallas_call(
        functools.partial(fused_kernel, n, half),
        out_shape=jax.ShapeDtypeStruct((n, 2, half, width), bf16),
        in_specs=[anywhere] * 3 + [in_vmem] * 2,
        out_specs=anywhere,
        scratch_shapes=[
            pltpu.VMEM((width, 3 * HALF_INNER), bf16),
            pltpu.VMEM((INNER, width), bf16),
            pltpu.VMEM((width, 3 * HALF_INNER), bf16),
            pltpu.VMEM((INNER, width), bf16),
            pltpu.VMEM((tracks, width), bf16),
            pltpu.VMEM((tracks, width), bf16),
            pltpu.VMEM((tracks, width), bf16),
            pltpu.VMEM((tokens, 3 * HALF_INNER), bf16),
            pltpu.VMEM((tracks, INNER), bf16),
            pltpu.VMEM((2, n, half, width), bf16),
            pltpu.VMEM((tracks, INNER), bf16),
            pltpu.VMEM((tracks, width), bf16),
            pltpu.VMEM((tracks, 3 * HALF_INNER), bf16),
            pltpu.VMEM((tracks, HALF_INNER), bf16),
            pltpu.VMEM((tracks, HALF_INNER), bf16),
            pltpu.VMEM((n, 2, half, width), bf16),
            dma((3,)),
            dma((3,)),
            dma((3,)),
            dma((3,)),
            dma((2,)),
            dma,
            dma((n,)),
            dma((n,)),
            dma((n,)),
            dma((n,)),
            dma,
            dma((2 * n,)),
            dma((2 * n,)),
            dma((2 * n,)),
            dma((2 * n,)),
            dma((2,)),
            dma((2,)),
            dma((blocks,)),
            dma((blocks,)),
            dma((blocks + 2,)),
        ],
        compiler_params=pltpu.CompilerParams(
            collective_id=0, has_side_effects=True, vmem_limit_bytes=56 * 1024 * 1024
        ),
        cost_estimate=pl.CostEstimate(
            flops=9_000_000_000, bytes_accessed=20_000_000, transcendentals=1_200_000
        ),
    )(
        tracks_in.reshape(tracks, width),
        w_qkv.reshape(width, 3 * INNER),
        w_out.reshape(INNER, width),
        visible.reshape(1, tracks),
        neighbours.reshape(blocks, NB).T,
    )
    return out.reshape(1, 1, 1, tracks, width)


def fits_fused(mesh):
    return mesh.shape["seq"] == FRAMES and mesh.shape["segment"] == 2


def solution(mesh):
    body = on_device_fused if fits_fused(mesh) else on_device
    return jax.shard_map(
        body,
        mesh=mesh,
        in_specs=(
            P(None, "seq", None, None),
            P("segment", None, None),
            P("segment", None, None),
            P(None, "seq", None),
            P(),
        ),
        out_specs=P("segment", None, "seq", None, None),
        check_vma=False,
    )
```

```python
import functools
import math

import jax
import jax.numpy as jnp
from jax import lax
from jax.experimental import pallas as pl
from jax.experimental.pallas import tpu as pltpu
from jax.sharding import PartitionSpec as P

HEADS = 6
HDIM = 128
BLOCK = 128
NB = 2
FRAMES = 16


epsilon = 1e-06


def partner(shard, axis, distance):
    return lax.ppermute(shard, axis, [(i, i ^ 1 << distance) for i in range(lax.axis_size(axis))])


def from_behind(value, axis, steps):
    count = lax.axis_size(axis)
    initial, last = (max(0, -steps), min(count, count - steps))
    return lax.ppermute(value, axis, [(source, source + steps) for source in range(initial, last)])


def normalize(tokens):
    widened = tokens.astype(jnp.float32)
    factor = lax.rsqrt(jnp.mean(widened * widened, axis=-1, keepdims=True) + epsilon)
    return (widened * factor).astype(jnp.bfloat16)


def project(tokens, weight):
    return jnp.dot(normalize(tokens), weight, preferred_element_type=jnp.float32).astype(
        jnp.bfloat16
    )


def finish(tokens, mixed_heads, weight):
    delta_rows = jnp.dot(mixed_heads, weight, preferred_element_type=jnp.float32)
    return (tokens.astype(jnp.float32) + delta_rows).astype(jnp.bfloat16)


def time_branch(projected, count, seq_size):
    inner = HEADS * HDIM
    shaped = projected.reshape(seq_size // FRAMES, FRAMES, count, 3, HEADS, HDIM)
    scores = jnp.einsum(
        "vfphd,vgphd->vphfg",
        shaped[:, :, :, 0],
        shaped[:, :, :, 1],
        preferred_element_type=jnp.float32,
    ) / math.sqrt(HDIM)
    exponent = jnp.exp(scores)
    weights = (exponent / jnp.sum(exponent, axis=-1, keepdims=True)).astype(jnp.bfloat16)
    mixed_heads = jnp.einsum(
        "vphfg,vgphd->vfphd", weights, shaped[:, :, :, 2], preferred_element_type=jnp.float32
    )
    return mixed_heads.reshape(-1, inner).astype(jnp.bfloat16)


def track_branch(projected, seen_mask, chosen, start_block, count):
    inner = HEADS * HDIM
    blocks_count = projected.shape[0] // BLOCK
    blocks_all = projected.reshape(blocks_count, BLOCK, 3, HEADS, HDIM)
    own_block = lax.broadcasted_iota(jnp.int32, (count, 1), 0) + start_block
    listing = jnp.concatenate(
        [own_block, lax.dynamic_slice_in_dim(chosen, start_block, count, 0)], axis=1
    )
    queries = lax.dynamic_slice_in_dim(blocks_all[:, :, 0], start_block, count, 0)
    keys_sel = jnp.take(blocks_all[:, :, 1], listing, axis=0)
    values_sel = jnp.take(blocks_all[:, :, 2], listing, axis=0)
    seen_sel = jnp.take(seen_mask.reshape(blocks_count, BLOCK), listing, axis=0)
    scores = jnp.einsum(
        "bqhd,bjkhd->bhqjk", queries, keys_sel, preferred_element_type=jnp.float32
    ) / math.sqrt(HDIM)
    shape_mask = (BLOCK, NB + 1, BLOCK)
    itself = (lax.broadcasted_iota(jnp.int32, shape_mask, 1) == 0) & (
        lax.broadcasted_iota(jnp.int32, shape_mask, 0)
        == lax.broadcasted_iota(jnp.int32, shape_mask, 2)
    )
    allowed = (seen_sel[:, None, None, :, :] == 1) | itself[None, None]
    exponent = jnp.where(allowed, jnp.exp(scores), jnp.zeros_like(scores))
    totals = jnp.sum(exponent, axis=(-2, -1), keepdims=True)
    weights = (exponent / totals).astype(jnp.bfloat16)
    mixed_heads = jnp.einsum(
        "bhqjk,bjkhd->bqhd", weights, values_sel, preferred_element_type=jnp.float32
    )
    return mixed_heads.reshape(count * BLOCK, inner).astype(jnp.bfloat16)


def on_device(tracks_in, w_qkv, w_out, visible, neighbours):
    segment_no = lax.axis_index("segment")
    seq_no = lax.axis_index("seq")
    seq_size = lax.axis_size("seq")
    segment_size = lax.axis_size("segment")
    tracks = tracks_in.shape[2]
    width = tracks_in.shape[3]
    per_device = tracks // seq_size
    blocks_count = tracks // BLOCK
    video_no = seq_no // FRAMES
    w_both, out_both = (
        lax.all_gather(w_qkv, "segment", axis=0, tiled=True),
        lax.all_gather(w_out, "segment", axis=0, tiled=True),
    )
    half = per_device // segment_size
    query_blocks = blocks_count // segment_size
    start_block = segment_no * query_blocks
    pieces = tracks_in[0, 0].reshape(seq_size, per_device, width)
    mine = lax.dynamic_slice_in_dim(pieces, segment_no * half, half, 1)
    moved = lax.all_to_all(mine, "seq", split_axis=0, concat_axis=0, tiled=True)
    flat = moved.reshape(seq_size * half, width)
    mixed_time = time_branch(project(flat, w_both[0]), half, seq_size)
    first_half = finish(flat, mixed_time, out_both[0]).reshape(seq_size, half, width)
    other_half = partner(first_half, "segment", 0)
    full_first = jnp.where(
        segment_no == 0,
        jnp.concatenate([first_half, other_half], axis=1),
        jnp.concatenate([other_half, first_half], axis=1),
    )
    frame_rows = lax.all_to_all(full_first, "seq", split_axis=0, concat_axis=0, tiled=True).reshape(
        tracks, width
    )
    projected = project(frame_rows, w_both[1])
    lists_now = lax.dynamic_index_in_dim(neighbours[0], video_no, 0, keepdims=False)
    mixed_track = track_branch(projected, visible[0, 0], lists_now, start_block, query_blocks)
    own_rows = lax.dynamic_slice_in_dim(frame_rows, start_block * BLOCK, query_blocks * BLOCK, 0)
    second_part = finish(own_rows, mixed_track, out_both[1])
    lower_part = from_behind(second_part, "segment", 1)
    full_second = jnp.concatenate([lower_part, second_part], axis=0)
    finals = [jnp.where(segment_no == 0, full_first.reshape(tracks, width), full_second)]
    return jnp.stack(finals)[None, :, None]


INNER = HEADS * HDIM
HALF_HEADS = HEADS // 2
HALF_INNER = HALF_HEADS * HDIM
MESH = pl.DeviceIdType.MESH
SCALE_LOG2 = math.log2(math.e) / math.sqrt(HDIM)


def dot(a, b):
    return jnp.dot(a, b, preferred_element_type=jnp.float32)


def dot_t(a, b):
    return lax.dot_general(a, b, (((1,), (1,)), ((), ())), preferred_element_type=jnp.float32)


def fused_kernel(
    n,
    half,
    x_ref,
    wq_ref,
    wo_ref,
    seen_ref,
    near_ref,
    out_ref,
    wq0,
    wo0,
    wq1,
    wo1,
    x_got,
    x_norm,
    x_frame,
    qkv0,
    mix0,
    first0,
    mix_frame,
    first1,
    qkv1,
    mix1,
    mix1_low,
    w_sem,
    w_send,
    x_send,
    x_recv,
    frame_sem,
    m_send,
    m_recv,
    f_send,
    f_recv,
    low_send,
    low_recv,
    out_send,
    out_recv,
):
    s = lax.axis_index("segment")
    me = lax.axis_index("seq")
    sibling = {"segment": 1 - s, "seq": me}
    group = 2 * half
    tokens = n * half
    tracks = n * group
    blocks = tracks // BLOCK

    def peer(d):
        return {"segment": s, "seq": d}

    def partner_at(k):
        bit, d = 1, 0
        while bit < n:
            mine = lax.rem(me // bit, 2)
            d = d + bit * lax.rem(mine + lax.rem(k // bit, 2), 2)
            bit *= 2
        return d

    barrier = pltpu.get_barrier_semaphore()

    def greet(k, c):
        pl.semaphore_signal(
            barrier, inc=1, device_id=peer(lax.rem(me + k, n)), device_id_type=MESH
        )
        return c

    lax.fori_loop(1, n, greet, 0)
    pl.semaphore_signal(barrier, inc=1, device_id=sibling, device_id_type=MESH)

    def rows(index, size):
        return pl.ds(pl.multiple_of(index * size, size), size)

    def x_copy(d, source):
        return pltpu.make_async_remote_copy(
            src_ref=x_ref.at[rows(2 * d + s, half), :],
            dst_ref=x_got.at[rows(source, half), :],
            send_sem=x_send.at[d],
            recv_sem=x_recv.at[source],
            device_id=peer(d),
            device_id_type=MESH,
        )

    def wq1_cols(core, j):
        return pl.ds(pl.multiple_of(j * INNER + core * HALF_INNER, HDIM), HALF_INNER)

    def wq1_dst(j):
        return wq1.at[:, pl.ds(j * HALF_INNER, HALF_INNER)]

    own_x = pltpu.make_async_copy(
        x_ref.at[rows(2 * me + s, half), :], x_got.at[rows(me, half), :], x_recv.at[me]
    )
    frame_copy = pltpu.make_async_copy(x_ref, x_frame, frame_sem)
    wq0_local = pltpu.make_async_copy(wq_ref, wq0, w_sem.at[0])
    wo0_local = pltpu.make_async_copy(wo_ref, wo0, w_sem.at[1])
    wo1_local = pltpu.make_async_copy(wo_ref, wo1, w_sem.at[2])
    wq1_local = [
        pltpu.make_async_copy(wq_ref.at[:, wq1_cols(s, j)], wq1_dst(j), w_sem.at[3 + j])
        for j in range(3)
    ]
    wq0_remote = pltpu.make_async_remote_copy(
        wq_ref, wq0, w_send.at[0], w_sem.at[0], device_id=sibling, device_id_type=MESH
    )
    wo0_remote = pltpu.make_async_remote_copy(
        wo_ref, wo0, w_send.at[1], w_sem.at[1], device_id=sibling, device_id_type=MESH
    )
    wq1_remote = [
        pltpu.make_async_remote_copy(
            wq_ref.at[:, wq1_cols(1 - s, j)],
            wq1_dst(j),
            w_send.at[2 + j],
            w_sem.at[3 + j],
            device_id=sibling,
            device_id_type=MESH,
        )
        for j in range(3)
    ]

    pl.semaphore_wait(barrier, n)

    def send_x(k, c):
        x_copy(partner_at(n - k), me).start()
        return c

    lax.fori_loop(1, n, send_x, 0)

    @pl.when(s == 0)
    def _():
        wq0_remote.start()
        wo0_remote.start()

    own_x.start()

    @pl.when(s == 0)
    def _():
        wq0_local.start()
        wo0_local.start()

    @pl.when(s == 1)
    def _():
        for copy in wq1_remote + wq1_local:
            copy.start()
        wo1_local.start()

    frame_copy.start()

    def norm_rows(k, c):
        source = partner_at(k)

        @pl.when(k > 0)
        def _():
            x_copy(source, source).wait_recv()

        @pl.when(k == 0)
        def _():
            own_x.wait()

        x_norm[rows(source, half), :] = normalize(x_got[rows(source, half), :])
        return c

    def project0(i, c):
        lax.fori_loop(i * (n // 2), (i + 1) * (n // 2), norm_rows, 0)

        @pl.when((i == 0) & (s == 0))
        def _():
            wq0_local.wait()

        @pl.when((i == 0) & (s == 1))
        def _():
            wq0_remote.wait_recv()

        part = rows(lax.rem(me // (n // 2) + i, 2), tokens // 2)
        qkv0[part, :] = dot(x_norm[part, :], wq0[...]).astype(jnp.bfloat16)
        return c

    lax.fori_loop(0, 2, project0, 0)

    i0 = lax.broadcasted_iota(jnp.int32, (tokens, tokens), 0)
    i1 = lax.broadcasted_iota(jnp.int32, (tokens, tokens), 1)
    same = lax.rem(i0, half) == lax.rem(i1, half)
    for h in range(HEADS):
        q = qkv0[:, h * HDIM : (h + 1) * HDIM]
        k = qkv0[:, INNER + h * HDIM : INNER + (h + 1) * HDIM]
        v = qkv0[:, 2 * INNER + h * HDIM : 2 * INNER + (h + 1) * HDIM]
        e = jnp.where(same, jnp.exp2(dot_t(q, k) * SCALE_LOG2), 0.0)
        w = (e * (1.0 / jnp.sum(e, axis=-1, keepdims=True))).astype(jnp.bfloat16)
        mix0[:, h * HDIM : (h + 1) * HDIM] = dot(w, v).astype(jnp.bfloat16)

    def m_copy(f, source):
        return pltpu.make_async_remote_copy(
            src_ref=mix0.at[rows(f, half), :],
            dst_ref=mix_frame.at[rows(s * n + source, half), :],
            send_sem=m_send.at[f],
            recv_sem=m_recv.at[source],
            device_id=peer(f),
            device_id_type=MESH,
        )

    per_block = BLOCK // group
    gathered = per_block * half

    def f_copy(b, core):
        place = rows(core * blocks + b, gathered)
        return pltpu.make_async_remote_copy(
            src_ref=mix_frame.at[place, :],
            dst_ref=mix_frame.at[place, :],
            send_sem=f_send.at[b],
            recv_sem=f_recv.at[b],
            device_id=sibling,
            device_id_type=MESH,
        )

    def send_m(k, c):
        m_copy(partner_at(n - k), me).start()
        return c

    lax.fori_loop(1, n, send_m, 0)
    mix_frame[rows(s * n + me, half), :] = mix0[rows(me, half), :]

    @pl.when(s == 0)
    def _():
        wo0_local.wait()

    @pl.when(s == 1)
    def _():
        wo0_remote.wait_recv()

    added = x_got[...].astype(jnp.float32) + dot(mix0[...], wo0[...])
    added = added.astype(jnp.bfloat16).reshape(n, half, -1)
    out_remote = pltpu.make_async_remote_copy(
        first0, out_ref.at[:, 1], out_send, out_recv, device_id=sibling, device_id_type=MESH
    )

    @pl.when(s == 0)
    def _():
        out_ref[:, 0] = added

    @pl.when(s == 1)
    def _():
        first0[...] = added
        out_remote.start()

    frame_copy.wait()
    for j in range(3):

        @pl.when(s == 0)
        def _():
            wq1_remote[j].wait_recv()

        @pl.when(s == 1)
        def _():
            wq1_local[j].wait()

    def middle(i, c):
        def arrive(k, c):
            source = partner_at(k)
            m_copy(source, source).wait_recv()
            return c

        lax.fori_loop(jnp.maximum(i * per_block, 1), (i + 1) * per_block, arrive, 0)
        b = partner_at(i * per_block) // per_block
        f_copy(b, s).start()
        f_copy(b, 1 - s).wait_recv()
        part = rows(b, BLOCK)
        halves = [
            mix_frame[rows(core * blocks + b, gathered), :].reshape(per_block, 1, half, INNER)
            for core in range(2)
        ]
        mixed = jnp.concatenate(halves, axis=1).reshape(BLOCK, INNER)
        grown = x_frame[part, :].astype(jnp.float32) + dot(mixed, wo0[...])
        grown = grown.astype(jnp.bfloat16)
        first1[part, :] = grown
        qkv1[part, :] = dot(normalize(grown), wq1[...]).astype(jnp.bfloat16)
        return c

    lax.fori_loop(0, blocks, middle, 0)

    r = lax.broadcasted_iota(jnp.int32, (BLOCK, tracks), 0)
    t = lax.broadcasted_iota(jnp.int32, (BLOCK, tracks), 1)
    track = lax.broadcasted_iota(jnp.int32, (1, tracks), 1)
    block_of = track // BLOCK
    near_at = lax.broadcasted_iota(jnp.int32, (NB, blocks), 1)
    seen = seen_ref[...] == 1

    def low_copy(b):
        return pltpu.make_async_remote_copy(
            src_ref=mix1.at[rows(b, BLOCK), :],
            dst_ref=mix1_low.at[rows(b, BLOCK), :],
            send_sem=low_send.at[b],
            recv_sem=low_recv.at[b],
            device_id=sibling,
            device_id_type=MESH,
        )

    def attend(b, c):
        part = rows(b, BLOCK)
        near = jnp.sum(jnp.where(near_at == b, near_ref[...], 0), axis=1, keepdims=True)
        listed = (block_of == b) | (block_of == near[0:1]) | (block_of == near[1:2])
        open_row = jnp.where(seen & listed, 1.0, 0.0)
        allow = jnp.where(t == r + b * BLOCK, 1.0, open_row) > 0.5
        for h in range(HALF_HEADS):
            q = qkv1[part, h * HDIM : (h + 1) * HDIM]
            k = qkv1[:, HALF_INNER + h * HDIM : HALF_INNER + (h + 1) * HDIM]
            v = qkv1[:, 2 * HALF_INNER + h * HDIM : 2 * HALF_INNER + (h + 1) * HDIM]
            e = jnp.where(allow, jnp.exp2(dot_t(q, k) * SCALE_LOG2), 0.0)
            w = (e * (1.0 / jnp.sum(e, axis=-1, keepdims=True))).astype(jnp.bfloat16)
            mix1[part, h * HDIM : (h + 1) * HDIM] = dot(w, v).astype(jnp.bfloat16)

        @pl.when(s == 0)
        def _():
            low_copy(b).start()

        return c

    lax.fori_loop(0, blocks, attend, 0)

    @pl.when(s == 1)
    def _():
        wo1_local.wait()

        def close(b, c):
            part = rows(b, BLOCK)
            low_copy(b).wait_recv()
            mixed = jnp.concatenate([mix1_low[part, :], mix1[part, :]], axis=1)
            total = first1[part, :].astype(jnp.float32) + dot(mixed, wo1[...])
            out_ref[rows(b, per_block)] = total.astype(jnp.bfloat16).reshape(
                per_block, 2, half, -1
            )
            return c

        lax.fori_loop(0, blocks, close, 0)
        out_remote.wait_send()
        for copy in wq1_remote:
            copy.wait_send()

    @pl.when(s == 0)
    def _():
        out_remote.wait_recv()
        wq0_remote.wait_send()
        wo0_remote.wait_send()

        def sent_low(b, c):
            low_copy(b).wait_send()
            return c

        lax.fori_loop(0, blocks, sent_low, 0)

    def drain(k, c):
        d = partner_at(k)
        x_copy(d, me).wait_send()
        m_copy(d, me).wait_send()
        return c

    lax.fori_loop(1, n, drain, 0)

    def drain_forwards(b, c):
        f_copy(b, s).wait_send()
        return c

    lax.fori_loop(0, blocks, drain_forwards, 0)


def on_device_fused(tracks_in, w_qkv, w_out, visible, neighbours):
    n = lax.axis_size("seq")
    tracks, width = tracks_in.shape[2:]
    half = tracks // n // 2
    tokens = n * half
    blocks = tracks // BLOCK
    bf16 = jnp.bfloat16
    dma = pltpu.SemaphoreType.DMA
    in_hbm = pl.BlockSpec(memory_space=pltpu.HBM)
    out = pl.pallas_call(
        functools.partial(fused_kernel, n, half),
        out_shape=jax.ShapeDtypeStruct((n, 2, half, width), bf16),
        in_specs=[in_hbm] * 3
        + [pl.BlockSpec(memory_space=pltpu.VMEM)] * 2,
        out_specs=pl.BlockSpec(memory_space=pltpu.VMEM),
        scratch_shapes=[
            pltpu.VMEM((width, 3 * INNER), bf16),
            pltpu.VMEM((INNER, width), bf16),
            pltpu.VMEM((width, 3 * HALF_INNER), bf16),
            pltpu.VMEM((INNER, width), bf16),
            pltpu.VMEM((tokens, width), bf16),
            pltpu.VMEM((tokens, width), bf16),
            pltpu.VMEM((tracks, width), bf16),
            pltpu.VMEM((tokens, 3 * INNER), bf16),
            pltpu.VMEM((tokens, INNER), bf16),
            pltpu.VMEM((n, half, width), bf16),
            pltpu.VMEM((tracks, INNER), bf16),
            pltpu.VMEM((tracks, width), bf16),
            pltpu.VMEM((tracks, 3 * HALF_INNER), bf16),
            pltpu.VMEM((tracks, HALF_INNER), bf16),
            pltpu.VMEM((tracks, HALF_INNER), bf16),
            dma((6,)),
            dma((5,)),
            dma((n,)),
            dma((n,)),
            dma,
            dma((n,)),
            dma((n,)),
            dma((blocks,)),
            dma((blocks,)),
            dma((blocks,)),
            dma((blocks,)),
            dma,
            dma,
        ],
        compiler_params=pltpu.CompilerParams(
            collective_id=0, has_side_effects=True, vmem_limit_bytes=32 * 1024 * 1024
        ),
        cost_estimate=pl.CostEstimate(
            flops=9_000_000_000, bytes_accessed=20_000_000, transcendentals=1_200_000
        ),
    )(
        tracks_in.reshape(tracks, width),
        w_qkv.reshape(width, 3 * INNER),
        w_out.reshape(INNER, width),
        visible.reshape(1, tracks),
        neighbours.reshape(blocks, NB).T,
    )
    return out.reshape(1, 1, 1, tracks, width)


def fits_fused(mesh):
    return mesh.shape["seq"] == FRAMES and mesh.shape["segment"] == 2


def solution(mesh):
    body = on_device_fused if fits_fused(mesh) else on_device
    return jax.shard_map(
        body,
        mesh=mesh,
        in_specs=(
            P(None, "seq", None, None),
            P("segment", None, None),
            P("segment", None, None),
            P(None, "seq", None),
            P(),
        ),
        out_specs=P("segment", None, "seq", None, None),
        check_vma=False,
    )
```

```python
import functools
import math

import jax
import jax.numpy as jnp
from jax import lax
from jax.experimental import pallas as pl
from jax.experimental.pallas import tpu as pltpu
from jax.sharding import PartitionSpec as P

HEADS = 6
HDIM = 128
BLOCK = 128
NB = 2
FRAMES = 16


epsilon = 1e-06


def partner(shard, axis, distance):
    return lax.ppermute(shard, axis, [(i, i ^ 1 << distance) for i in range(lax.axis_size(axis))])


def from_behind(value, axis, steps):
    count = lax.axis_size(axis)
    initial, last = (max(0, -steps), min(count, count - steps))
    return lax.ppermute(value, axis, [(source, source + steps) for source in range(initial, last)])


def normalize(tokens):
    widened = tokens.astype(jnp.float32)
    factor = lax.rsqrt(jnp.mean(widened * widened, axis=-1, keepdims=True) + epsilon)
    return (widened * factor).astype(jnp.bfloat16)


def project(tokens, weight):
    return jnp.dot(normalize(tokens), weight, preferred_element_type=jnp.float32).astype(
        jnp.bfloat16
    )


def finish(tokens, mixed_heads, weight):
    delta_rows = jnp.dot(mixed_heads, weight, preferred_element_type=jnp.float32)
    return (tokens.astype(jnp.float32) + delta_rows).astype(jnp.bfloat16)


def time_branch(projected, count, seq_size):
    inner = HEADS * HDIM
    shaped = projected.reshape(seq_size // FRAMES, FRAMES, count, 3, HEADS, HDIM)
    scores = jnp.einsum(
        "vfphd,vgphd->vphfg",
        shaped[:, :, :, 0],
        shaped[:, :, :, 1],
        preferred_element_type=jnp.float32,
    ) / math.sqrt(HDIM)
    exponent = jnp.exp(scores)
    weights = (exponent / jnp.sum(exponent, axis=-1, keepdims=True)).astype(jnp.bfloat16)
    mixed_heads = jnp.einsum(
        "vphfg,vgphd->vfphd", weights, shaped[:, :, :, 2], preferred_element_type=jnp.float32
    )
    return mixed_heads.reshape(-1, inner).astype(jnp.bfloat16)


def track_branch(projected, seen_mask, chosen, start_block, count):
    inner = HEADS * HDIM
    blocks_count = projected.shape[0] // BLOCK
    blocks_all = projected.reshape(blocks_count, BLOCK, 3, HEADS, HDIM)
    own_block = lax.broadcasted_iota(jnp.int32, (count, 1), 0) + start_block
    listing = jnp.concatenate(
        [own_block, lax.dynamic_slice_in_dim(chosen, start_block, count, 0)], axis=1
    )
    queries = lax.dynamic_slice_in_dim(blocks_all[:, :, 0], start_block, count, 0)
    keys_sel = jnp.take(blocks_all[:, :, 1], listing, axis=0)
    values_sel = jnp.take(blocks_all[:, :, 2], listing, axis=0)
    seen_sel = jnp.take(seen_mask.reshape(blocks_count, BLOCK), listing, axis=0)
    scores = jnp.einsum(
        "bqhd,bjkhd->bhqjk", queries, keys_sel, preferred_element_type=jnp.float32
    ) / math.sqrt(HDIM)
    shape_mask = (BLOCK, NB + 1, BLOCK)
    itself = (lax.broadcasted_iota(jnp.int32, shape_mask, 1) == 0) & (
        lax.broadcasted_iota(jnp.int32, shape_mask, 0)
        == lax.broadcasted_iota(jnp.int32, shape_mask, 2)
    )
    allowed = (seen_sel[:, None, None, :, :] == 1) | itself[None, None]
    exponent = jnp.where(allowed, jnp.exp(scores), jnp.zeros_like(scores))
    totals = jnp.sum(exponent, axis=(-2, -1), keepdims=True)
    weights = (exponent / totals).astype(jnp.bfloat16)
    mixed_heads = jnp.einsum(
        "bhqjk,bjkhd->bqhd", weights, values_sel, preferred_element_type=jnp.float32
    )
    return mixed_heads.reshape(count * BLOCK, inner).astype(jnp.bfloat16)


def on_device(tracks_in, w_qkv, w_out, visible, neighbours):
    segment_no = lax.axis_index("segment")
    seq_no = lax.axis_index("seq")
    seq_size = lax.axis_size("seq")
    segment_size = lax.axis_size("segment")
    tracks = tracks_in.shape[2]
    width = tracks_in.shape[3]
    per_device = tracks // seq_size
    blocks_count = tracks // BLOCK
    video_no = seq_no // FRAMES
    w_both, out_both = (
        lax.all_gather(w_qkv, "segment", axis=0, tiled=True),
        lax.all_gather(w_out, "segment", axis=0, tiled=True),
    )
    half = per_device // segment_size
    query_blocks = blocks_count // segment_size
    start_block = segment_no * query_blocks
    pieces = tracks_in[0, 0].reshape(seq_size, per_device, width)
    mine = lax.dynamic_slice_in_dim(pieces, segment_no * half, half, 1)
    moved = lax.all_to_all(mine, "seq", split_axis=0, concat_axis=0, tiled=True)
    flat = moved.reshape(seq_size * half, width)
    mixed_time = time_branch(project(flat, w_both[0]), half, seq_size)
    first_half = finish(flat, mixed_time, out_both[0]).reshape(seq_size, half, width)
    other_half = partner(first_half, "segment", 0)
    full_first = jnp.where(
        segment_no == 0,
        jnp.concatenate([first_half, other_half], axis=1),
        jnp.concatenate([other_half, first_half], axis=1),
    )
    frame_rows = lax.all_to_all(full_first, "seq", split_axis=0, concat_axis=0, tiled=True).reshape(
        tracks, width
    )
    projected = project(frame_rows, w_both[1])
    lists_now = lax.dynamic_index_in_dim(neighbours[0], video_no, 0, keepdims=False)
    mixed_track = track_branch(projected, visible[0, 0], lists_now, start_block, query_blocks)
    own_rows = lax.dynamic_slice_in_dim(frame_rows, start_block * BLOCK, query_blocks * BLOCK, 0)
    second_part = finish(own_rows, mixed_track, out_both[1])
    lower_part = from_behind(second_part, "segment", 1)
    full_second = jnp.concatenate([lower_part, second_part], axis=0)
    finals = [jnp.where(segment_no == 0, full_first.reshape(tracks, width), full_second)]
    return jnp.stack(finals)[None, :, None]


INNER = HEADS * HDIM
HALF_HEADS = HEADS // 2
HALF_INNER = HALF_HEADS * HDIM
MESH = pl.DeviceIdType.MESH
MASKED = -1e30
SCALE_LOG2 = math.log2(math.e) / math.sqrt(HDIM)


def dot(a, b):
    return jnp.dot(a, b, preferred_element_type=jnp.float32)


def dot_t(a, b):
    return lax.dot_general(a, b, (((1,), (1,)), ((), ())), preferred_element_type=jnp.float32)


def fused_kernel(
    n,
    half,
    x_ref,
    wq_ref,
    wo_ref,
    seen_ref,
    near_ref,
    out_ref,
    wq0,
    wo0,
    wq1,
    wo1,
    x_got,
    x_norm,
    x_frame,
    qkv0,
    mix0,
    first0,
    mix_frame,
    first1,
    qkv1,
    mix1,
    mix1_low,
    bias0,
    bias1,
    w_sem,
    w_send,
    x_send,
    x_recv,
    frame_sem,
    m_send,
    m_recv,
    f_send,
    f_recv,
    low_send,
    low_recv,
    out_send,
    out_recv,
):
    s = lax.axis_index("segment")
    me = lax.axis_index("seq")
    sibling = {"segment": 1 - s, "seq": me}
    group = 2 * half
    tokens = n * half
    tracks = n * group
    blocks = tracks // BLOCK

    def peer(d):
        return {"segment": s, "seq": d}

    def partner_at(k):
        bit, d = 1, 0
        while bit < n:
            mine = lax.rem(me // bit, 2)
            d = d + bit * lax.rem(mine + lax.rem(k // bit, 2), 2)
            bit *= 2
        return d

    barrier = pltpu.get_barrier_semaphore()

    def greet(k, c):
        pl.semaphore_signal(
            barrier, inc=1, device_id=peer(lax.rem(me + k, n)), device_id_type=MESH
        )
        return c

    lax.fori_loop(1, n, greet, 0)
    pl.semaphore_signal(barrier, inc=1, device_id=sibling, device_id_type=MESH)

    def rows(index, size):
        return pl.ds(pl.multiple_of(index * size, size), size)

    def x_copy(d, source):
        return pltpu.make_async_remote_copy(
            src_ref=x_ref.at[rows(2 * d + s, half), :],
            dst_ref=x_got.at[rows(source, half), :],
            send_sem=x_send.at[d],
            recv_sem=x_recv.at[source],
            device_id=peer(d),
            device_id_type=MESH,
        )

    def wq1_cols(core, j):
        return pl.ds(pl.multiple_of(j * INNER + core * HALF_INNER, HDIM), HALF_INNER)

    def wq1_dst(j):
        return wq1.at[:, pl.ds(j * HALF_INNER, HALF_INNER)]

    own_x = pltpu.make_async_copy(
        x_ref.at[rows(2 * me + s, half), :], x_got.at[rows(me, half), :], x_recv.at[me]
    )
    frame_copy = pltpu.make_async_copy(x_ref, x_frame, frame_sem)
    wq0_local = pltpu.make_async_copy(wq_ref, wq0, w_sem.at[0])
    wo0_local = pltpu.make_async_copy(wo_ref, wo0, w_sem.at[1])
    wo1_local = pltpu.make_async_copy(wo_ref, wo1, w_sem.at[2])
    wq1_local = [
        pltpu.make_async_copy(wq_ref.at[:, wq1_cols(s, j)], wq1_dst(j), w_sem.at[3 + j])
        for j in range(3)
    ]
    wq0_remote = pltpu.make_async_remote_copy(
        wq_ref, wq0, w_send.at[0], w_sem.at[0], device_id=sibling, device_id_type=MESH
    )
    wo0_remote = pltpu.make_async_remote_copy(
        wo_ref, wo0, w_send.at[1], w_sem.at[1], device_id=sibling, device_id_type=MESH
    )
    wq1_remote = [
        pltpu.make_async_remote_copy(
            wq_ref.at[:, wq1_cols(1 - s, j)],
            wq1_dst(j),
            w_send.at[2 + j],
            w_sem.at[3 + j],
            device_id=sibling,
            device_id_type=MESH,
        )
        for j in range(3)
    ]

    pl.semaphore_wait(barrier, n)

    def send_x(k, c):
        x_copy(partner_at(n - k), me).start()
        return c

    lax.fori_loop(1, n, send_x, 0)

    @pl.when(s == 0)
    def _():
        wq0_remote.start()
        wo0_remote.start()

    own_x.start()

    @pl.when(s == 0)
    def _():
        wq0_local.start()
        wo0_local.start()

    @pl.when(s == 1)
    def _():
        for copy in wq1_remote + wq1_local:
            copy.start()
        wo1_local.start()

    frame_copy.start()

    i0 = lax.broadcasted_iota(jnp.int32, (tokens, tokens), 0)
    i1 = lax.broadcasted_iota(jnp.int32, (tokens, tokens), 1)
    bias0[...] = jnp.where(lax.rem(i0, half) == lax.rem(i1, half), 0.0, MASKED)
    r = lax.broadcasted_iota(jnp.int32, (BLOCK, tracks), 0)
    t = lax.broadcasted_iota(jnp.int32, (BLOCK, tracks), 1)
    block_of = lax.broadcasted_iota(jnp.int32, (1, tracks), 1) // BLOCK
    seen = seen_ref[...] == 1
    for b in range(blocks):
        listed = block_of == b
        for j in range(NB):
            listed = listed | (block_of == near_ref[j : j + 1, b : b + 1])
        open_row = jnp.where(seen & listed, 0.0, MASKED)
        bias1[b * BLOCK : (b + 1) * BLOCK, :] = jnp.where(t == r + b * BLOCK, 0.0, open_row)

    def norm_rows(k, c):
        source = partner_at(k)

        @pl.when(k > 0)
        def _():
            x_copy(source, source).wait_recv()

        @pl.when(k == 0)
        def _():
            own_x.wait()

        x_norm[rows(source, half), :] = normalize(x_got[rows(source, half), :])
        return c

    def project0(i, c):
        lax.fori_loop(i * (n // 2), (i + 1) * (n // 2), norm_rows, 0)

        @pl.when((i == 0) & (s == 0))
        def _():
            wq0_local.wait()

        @pl.when((i == 0) & (s == 1))
        def _():
            wq0_remote.wait_recv()

        part = rows(lax.rem(me // (n // 2) + i, 2), tokens // 2)
        qkv0[part, :] = dot(x_norm[part, :], wq0[...]).astype(jnp.bfloat16)
        return c

    lax.fori_loop(0, 2, project0, 0)

    for h in range(HEADS):
        q = qkv0[:, h * HDIM : (h + 1) * HDIM]
        k = qkv0[:, INNER + h * HDIM : INNER + (h + 1) * HDIM]
        v = qkv0[:, 2 * INNER + h * HDIM : 2 * INNER + (h + 1) * HDIM]
        e = jnp.exp2(dot_t(q, k) * SCALE_LOG2 + bias0[...])
        w = (e * (1.0 / jnp.sum(e, axis=-1, keepdims=True))).astype(jnp.bfloat16)
        mix0[:, h * HDIM : (h + 1) * HDIM] = dot(w, v).astype(jnp.bfloat16)

    def m_copy(f, source):
        return pltpu.make_async_remote_copy(
            src_ref=mix0.at[rows(f, half), :],
            dst_ref=mix_frame.at[rows(s * n + source, half), :],
            send_sem=m_send.at[f],
            recv_sem=m_recv.at[source],
            device_id=peer(f),
            device_id_type=MESH,
        )

    per_block = BLOCK // group
    gathered = per_block * half

    def f_copy(b, core):
        place = rows(core * blocks + b, gathered)
        return pltpu.make_async_remote_copy(
            src_ref=mix_frame.at[place, :],
            dst_ref=mix_frame.at[place, :],
            send_sem=f_send.at[b],
            recv_sem=f_recv.at[b],
            device_id=sibling,
            device_id_type=MESH,
        )

    def send_m(k, c):
        m_copy(partner_at(n - k), me).start()
        return c

    lax.fori_loop(1, n, send_m, 0)
    mix_frame[rows(s * n + me, half), :] = mix0[rows(me, half), :]

    @pl.when(s == 0)
    def _():
        wo0_local.wait()

    @pl.when(s == 1)
    def _():
        wo0_remote.wait_recv()

    added = x_got[...].astype(jnp.float32) + dot(mix0[...], wo0[...])
    added = added.astype(jnp.bfloat16).reshape(n, half, -1)
    out_remote = pltpu.make_async_remote_copy(
        first0, out_ref.at[:, 1], out_send, out_recv, device_id=sibling, device_id_type=MESH
    )

    @pl.when(s == 0)
    def _():
        out_ref[:, 0] = added

    @pl.when(s == 1)
    def _():
        first0[...] = added
        out_remote.start()

    frame_copy.wait()
    for j in range(3):

        @pl.when(s == 0)
        def _():
            wq1_remote[j].wait_recv()

        @pl.when(s == 1)
        def _():
            wq1_local[j].wait()

    def middle(i, c):
        def arrive(k, c):
            source = partner_at(k)
            m_copy(source, source).wait_recv()
            return c

        lax.fori_loop(jnp.maximum(i * per_block, 1), (i + 1) * per_block, arrive, 0)
        b = partner_at(i * per_block) // per_block
        f_copy(b, s).start()
        f_copy(b, 1 - s).wait_recv()
        part = rows(b, BLOCK)
        halves = [
            mix_frame[rows(core * blocks + b, gathered), :].reshape(per_block, 1, half, INNER)
            for core in range(2)
        ]
        mixed = jnp.concatenate(halves, axis=1).reshape(BLOCK, INNER)
        grown = x_frame[part, :].astype(jnp.float32) + dot(mixed, wo0[...])
        grown = grown.astype(jnp.bfloat16)
        first1[part, :] = grown
        qkv1[part, :] = dot(normalize(grown), wq1[...]).astype(jnp.bfloat16)
        return c

    lax.fori_loop(0, blocks, middle, 0)

    span = tracks // 2

    def low_copy(i):
        place = pl.ds(i * span, span)
        return pltpu.make_async_remote_copy(
            src_ref=mix1.at[place, :],
            dst_ref=mix1_low.at[place, :],
            send_sem=low_send.at[i],
            recv_sem=low_recv.at[i],
            device_id=sibling,
            device_id_type=MESH,
        )

    for i in range(2):
        part = slice(i * span, (i + 1) * span)
        for h in range(HALF_HEADS):
            q = qkv1[part, h * HDIM : (h + 1) * HDIM]
            k = qkv1[:, HALF_INNER + h * HDIM : HALF_INNER + (h + 1) * HDIM]
            v = qkv1[:, 2 * HALF_INNER + h * HDIM : 2 * HALF_INNER + (h + 1) * HDIM]
            e = jnp.exp2(dot_t(q, k) * SCALE_LOG2 + bias1[part, :])
            w = (e * (1.0 / jnp.sum(e, axis=-1, keepdims=True))).astype(jnp.bfloat16)
            mix1[part, h * HDIM : (h + 1) * HDIM] = dot(w, v).astype(jnp.bfloat16)

        @pl.when(s == 0)
        def _():
            low_copy(i).start()

    @pl.when(s == 1)
    def _():
        wo1_local.wait()
        for i in range(2):
            part = slice(i * span, (i + 1) * span)
            low_copy(i).wait_recv()
            mixed = jnp.concatenate([mix1_low[part, :], mix1[part, :]], axis=1)
            total = first1[part, :].astype(jnp.float32) + dot(mixed, wo1[...])
            out_ref[i * n // 2 : (i + 1) * n // 2] = total.astype(jnp.bfloat16).reshape(
                n // 2, 2, half, -1
            )
        out_remote.wait_send()
        for copy in wq1_remote:
            copy.wait_send()

    @pl.when(s == 0)
    def _():
        out_remote.wait_recv()
        wq0_remote.wait_send()
        wo0_remote.wait_send()

        for i in range(2):
            low_copy(i).wait_send()

    def drain(k, c):
        d = partner_at(k)
        x_copy(d, me).wait_send()
        m_copy(d, me).wait_send()
        return c

    lax.fori_loop(1, n, drain, 0)

    def drain_forwards(b, c):
        f_copy(b, s).wait_send()
        return c

    lax.fori_loop(0, blocks, drain_forwards, 0)


def on_device_fused(tracks_in, w_qkv, w_out, visible, neighbours):
    n = lax.axis_size("seq")
    tracks, width = tracks_in.shape[2:]
    half = tracks // n // 2
    tokens = n * half
    blocks = tracks // BLOCK
    bf16 = jnp.bfloat16
    dma = pltpu.SemaphoreType.DMA
    in_hbm = pl.BlockSpec(memory_space=pltpu.HBM)
    out = pl.pallas_call(
        functools.partial(fused_kernel, n, half),
        out_shape=jax.ShapeDtypeStruct((n, 2, half, width), bf16),
        in_specs=[in_hbm] * 3
        + [pl.BlockSpec(memory_space=pltpu.VMEM)] * 2,
        out_specs=pl.BlockSpec(memory_space=pltpu.VMEM),
        scratch_shapes=[
            pltpu.VMEM((width, 3 * INNER), bf16),
            pltpu.VMEM((INNER, width), bf16),
            pltpu.VMEM((width, 3 * HALF_INNER), bf16),
            pltpu.VMEM((INNER, width), bf16),
            pltpu.VMEM((tokens, width), bf16),
            pltpu.VMEM((tokens, width), bf16),
            pltpu.VMEM((tracks, width), bf16),
            pltpu.VMEM((tokens, 3 * INNER), bf16),
            pltpu.VMEM((tokens, INNER), bf16),
            pltpu.VMEM((n, half, width), bf16),
            pltpu.VMEM((tracks, INNER), bf16),
            pltpu.VMEM((tracks, width), bf16),
            pltpu.VMEM((tracks, 3 * HALF_INNER), bf16),
            pltpu.VMEM((tracks, HALF_INNER), bf16),
            pltpu.VMEM((tracks, HALF_INNER), bf16),
            pltpu.VMEM((tokens, tokens), jnp.float32),
            pltpu.VMEM((tracks, tracks), jnp.float32),
            dma((6,)),
            dma((5,)),
            dma((n,)),
            dma((n,)),
            dma,
            dma((n,)),
            dma((n,)),
            dma((blocks,)),
            dma((blocks,)),
            dma((blocks,)),
            dma((blocks,)),
            dma,
            dma,
        ],
        compiler_params=pltpu.CompilerParams(
            collective_id=0, has_side_effects=True, vmem_limit_bytes=52 * 1024 * 1024
        ),
        cost_estimate=pl.CostEstimate(
            flops=9_000_000_000, bytes_accessed=20_000_000, transcendentals=1_200_000
        ),
    )(
        tracks_in.reshape(tracks, width),
        w_qkv.reshape(width, 3 * INNER),
        w_out.reshape(INNER, width),
        visible.reshape(1, tracks),
        neighbours.reshape(blocks, NB).T,
    )
    return out.reshape(1, 1, 1, tracks, width)


def fits_fused(mesh):
    return mesh.shape["seq"] == FRAMES and mesh.shape["segment"] == 2


def solution(mesh):
    body = on_device_fused if fits_fused(mesh) else on_device
    return jax.shard_map(
        body,
        mesh=mesh,
        in_specs=(
            P(None, "seq", None, None),
            P("segment", None, None),
            P("segment", None, None),
            P(None, "seq", None),
            P(),
        ),
        out_specs=P("segment", None, "seq", None, None),
        check_vma=False,
    )
```

```python
import functools
import math

import jax
import jax.numpy as jnp
from jax import lax
from jax.experimental import pallas as pl
from jax.experimental.pallas import tpu as pltpu
from jax.sharding import PartitionSpec as P

HEADS = 6
HDIM = 128
BLOCK = 128
NB = 2
FRAMES = 16


epsilon = 1e-06


def partner(shard, axis, distance):
    return lax.ppermute(shard, axis, [(i, i ^ 1 << distance) for i in range(lax.axis_size(axis))])


def from_behind(value, axis, steps):
    count = lax.axis_size(axis)
    initial, last = (max(0, -steps), min(count, count - steps))
    return lax.ppermute(value, axis, [(source, source + steps) for source in range(initial, last)])


def normalize(tokens):
    widened = tokens.astype(jnp.float32)
    factor = lax.rsqrt(jnp.mean(widened * widened, axis=-1, keepdims=True) + epsilon)
    return (widened * factor).astype(jnp.bfloat16)


def project(tokens, weight):
    return jnp.dot(normalize(tokens), weight, preferred_element_type=jnp.float32).astype(
        jnp.bfloat16
    )


def finish(tokens, mixed_heads, weight):
    delta_rows = jnp.dot(mixed_heads, weight, preferred_element_type=jnp.float32)
    return (tokens.astype(jnp.float32) + delta_rows).astype(jnp.bfloat16)


def time_branch(projected, count, seq_size):
    inner = HEADS * HDIM
    shaped = projected.reshape(seq_size // FRAMES, FRAMES, count, 3, HEADS, HDIM)
    scores = jnp.einsum(
        "vfphd,vgphd->vphfg",
        shaped[:, :, :, 0],
        shaped[:, :, :, 1],
        preferred_element_type=jnp.float32,
    ) / math.sqrt(HDIM)
    exponent = jnp.exp(scores)
    weights = (exponent / jnp.sum(exponent, axis=-1, keepdims=True)).astype(jnp.bfloat16)
    mixed_heads = jnp.einsum(
        "vphfg,vgphd->vfphd", weights, shaped[:, :, :, 2], preferred_element_type=jnp.float32
    )
    return mixed_heads.reshape(-1, inner).astype(jnp.bfloat16)


def track_branch(projected, seen_mask, chosen, start_block, count):
    inner = HEADS * HDIM
    blocks_count = projected.shape[0] // BLOCK
    blocks_all = projected.reshape(blocks_count, BLOCK, 3, HEADS, HDIM)
    own_block = lax.broadcasted_iota(jnp.int32, (count, 1), 0) + start_block
    listing = jnp.concatenate(
        [own_block, lax.dynamic_slice_in_dim(chosen, start_block, count, 0)], axis=1
    )
    queries = lax.dynamic_slice_in_dim(blocks_all[:, :, 0], start_block, count, 0)
    keys_sel = jnp.take(blocks_all[:, :, 1], listing, axis=0)
    values_sel = jnp.take(blocks_all[:, :, 2], listing, axis=0)
    seen_sel = jnp.take(seen_mask.reshape(blocks_count, BLOCK), listing, axis=0)
    scores = jnp.einsum(
        "bqhd,bjkhd->bhqjk", queries, keys_sel, preferred_element_type=jnp.float32
    ) / math.sqrt(HDIM)
    shape_mask = (BLOCK, NB + 1, BLOCK)
    itself = (lax.broadcasted_iota(jnp.int32, shape_mask, 1) == 0) & (
        lax.broadcasted_iota(jnp.int32, shape_mask, 0)
        == lax.broadcasted_iota(jnp.int32, shape_mask, 2)
    )
    allowed = (seen_sel[:, None, None, :, :] == 1) | itself[None, None]
    exponent = jnp.where(allowed, jnp.exp(scores), jnp.zeros_like(scores))
    totals = jnp.sum(exponent, axis=(-2, -1), keepdims=True)
    weights = (exponent / totals).astype(jnp.bfloat16)
    mixed_heads = jnp.einsum(
        "bhqjk,bjkhd->bqhd", weights, values_sel, preferred_element_type=jnp.float32
    )
    return mixed_heads.reshape(count * BLOCK, inner).astype(jnp.bfloat16)


def on_device(tracks_in, w_qkv, w_out, visible, neighbours):
    segment_no = lax.axis_index("segment")
    seq_no = lax.axis_index("seq")
    seq_size = lax.axis_size("seq")
    segment_size = lax.axis_size("segment")
    tracks = tracks_in.shape[2]
    width = tracks_in.shape[3]
    per_device = tracks // seq_size
    blocks_count = tracks // BLOCK
    video_no = seq_no // FRAMES
    w_both, out_both = (
        lax.all_gather(w_qkv, "segment", axis=0, tiled=True),
        lax.all_gather(w_out, "segment", axis=0, tiled=True),
    )
    half = per_device // segment_size
    query_blocks = blocks_count // segment_size
    start_block = segment_no * query_blocks
    pieces = tracks_in[0, 0].reshape(seq_size, per_device, width)
    mine = lax.dynamic_slice_in_dim(pieces, segment_no * half, half, 1)
    moved = lax.all_to_all(mine, "seq", split_axis=0, concat_axis=0, tiled=True)
    flat = moved.reshape(seq_size * half, width)
    mixed_time = time_branch(project(flat, w_both[0]), half, seq_size)
    first_half = finish(flat, mixed_time, out_both[0]).reshape(seq_size, half, width)
    other_half = partner(first_half, "segment", 0)
    full_first = jnp.where(
        segment_no == 0,
        jnp.concatenate([first_half, other_half], axis=1),
        jnp.concatenate([other_half, first_half], axis=1),
    )
    frame_rows = lax.all_to_all(full_first, "seq", split_axis=0, concat_axis=0, tiled=True).reshape(
        tracks, width
    )
    projected = project(frame_rows, w_both[1])
    lists_now = lax.dynamic_index_in_dim(neighbours[0], video_no, 0, keepdims=False)
    mixed_track = track_branch(projected, visible[0, 0], lists_now, start_block, query_blocks)
    own_rows = lax.dynamic_slice_in_dim(frame_rows, start_block * BLOCK, query_blocks * BLOCK, 0)
    second_part = finish(own_rows, mixed_track, out_both[1])
    lower_part = from_behind(second_part, "segment", 1)
    full_second = jnp.concatenate([lower_part, second_part], axis=0)
    finals = [jnp.where(segment_no == 0, full_first.reshape(tracks, width), full_second)]
    return jnp.stack(finals)[None, :, None]


INNER = HEADS * HDIM
HALF_HEADS = HEADS // 2
HALF_INNER = HALF_HEADS * HDIM
MESH = pl.DeviceIdType.MESH
MASKED = -1e30
SCALE_LOG2 = math.log2(math.e) / math.sqrt(HDIM)


def dot(a, b):
    return jnp.dot(a, b, preferred_element_type=jnp.float32)


def dot_t(a, b):
    return lax.dot_general(a, b, (((1,), (1,)), ((), ())), preferred_element_type=jnp.float32)


def fused_kernel(
    n,
    half,
    x_ref,
    wq_ref,
    wo_ref,
    seen_ref,
    near_ref,
    out_ref,
    wq0,
    wo0,
    wq1,
    wo1,
    x_got,
    x_norm,
    x_frame,
    qkv0,
    mix0,
    first0,
    mix_frame,
    first1,
    qkv1,
    mix1,
    mix1_low,
    bias0,
    bias1,
    w_sem,
    w_send,
    x_send,
    x_recv,
    frame_sem,
    m_send,
    m_recv,
    f_send,
    f_recv,
    low_send,
    low_recv,
    out_send,
    out_recv,
):
    s = lax.axis_index("segment")
    me = lax.axis_index("seq")
    sibling = {"segment": 1 - s, "seq": me}
    group = 2 * half
    tokens = n * half
    tracks = n * group
    blocks = tracks // BLOCK

    def peer(d):
        return {"segment": s, "seq": d}

    def partner_at(k):
        bit, d = 1, 0
        while bit < n:
            mine = lax.rem(me // bit, 2)
            d = d + bit * lax.rem(mine + lax.rem(k // bit, 2), 2)
            bit *= 2
        return d

    barrier = pltpu.get_barrier_semaphore()

    def greet(k, c):
        pl.semaphore_signal(
            barrier, inc=1, device_id=peer(lax.rem(me + k, n)), device_id_type=MESH
        )
        return c

    lax.fori_loop(1, n, greet, 0)
    pl.semaphore_signal(barrier, inc=1, device_id=sibling, device_id_type=MESH)

    def rows(index, size):
        return pl.ds(pl.multiple_of(index * size, size), size)

    def x_copy(d, source):
        return pltpu.make_async_remote_copy(
            src_ref=x_ref.at[rows(2 * d + s, half), :],
            dst_ref=x_got.at[rows(source, half), :],
            send_sem=x_send.at[d],
            recv_sem=x_recv.at[source],
            device_id=peer(d),
            device_id_type=MESH,
        )

    def wq1_cols(core, j):
        return pl.ds(pl.multiple_of(j * INNER + core * HALF_INNER, HDIM), HALF_INNER)

    def wq1_dst(j):
        return wq1.at[:, pl.ds(j * HALF_INNER, HALF_INNER)]

    own_x = pltpu.make_async_copy(
        x_ref.at[rows(2 * me + s, half), :], x_got.at[rows(me, half), :], x_recv.at[me]
    )
    frame_copy = pltpu.make_async_copy(x_ref, x_frame, frame_sem)
    wq0_local = pltpu.make_async_copy(wq_ref, wq0, w_sem.at[0])
    wo0_local = pltpu.make_async_copy(wo_ref, wo0, w_sem.at[1])
    wo1_local = pltpu.make_async_copy(wo_ref, wo1, w_sem.at[2])
    wq1_local = [
        pltpu.make_async_copy(wq_ref.at[:, wq1_cols(s, j)], wq1_dst(j), w_sem.at[3 + j])
        for j in range(3)
    ]
    wq0_remote = pltpu.make_async_remote_copy(
        wq_ref, wq0, w_send.at[0], w_sem.at[0], device_id=sibling, device_id_type=MESH
    )
    wo0_remote = pltpu.make_async_remote_copy(
        wo_ref, wo0, w_send.at[1], w_sem.at[1], device_id=sibling, device_id_type=MESH
    )
    wq1_remote = [
        pltpu.make_async_remote_copy(
            wq_ref.at[:, wq1_cols(1 - s, j)],
            wq1_dst(j),
            w_send.at[2 + j],
            w_sem.at[3 + j],
            device_id=sibling,
            device_id_type=MESH,
        )
        for j in range(3)
    ]

    pl.semaphore_wait(barrier, n)

    def send_x(k, c):
        x_copy(partner_at(n - k), me).start()
        return c

    lax.fori_loop(1, n, send_x, 0)

    @pl.when(s == 0)
    def _():
        wq0_remote.start()
        wo0_remote.start()

    own_x.start()

    @pl.when(s == 0)
    def _():
        wq0_local.start()
        wo0_local.start()

    @pl.when(s == 1)
    def _():
        for copy in wq1_remote + wq1_local:
            copy.start()
        wo1_local.start()

    frame_copy.start()

    i0 = lax.broadcasted_iota(jnp.int32, (tokens, tokens), 0)
    i1 = lax.broadcasted_iota(jnp.int32, (tokens, tokens), 1)
    bias0[...] = jnp.where(lax.rem(i0, half) == lax.rem(i1, half), 0.0, MASKED)
    r = lax.broadcasted_iota(jnp.int32, (BLOCK, tracks), 0)
    t = lax.broadcasted_iota(jnp.int32, (BLOCK, tracks), 1)
    block_of = lax.broadcasted_iota(jnp.int32, (1, tracks), 1) // BLOCK
    seen = seen_ref[...] == 1
    for b in range(blocks):
        listed = block_of == b
        for j in range(NB):
            listed = listed | (block_of == near_ref[j : j + 1, b : b + 1])
        open_row = jnp.where(seen & listed, 0.0, MASKED)
        bias1[b * BLOCK : (b + 1) * BLOCK, :] = jnp.where(t == r + b * BLOCK, 0.0, open_row)

    def norm_rows(k, c):
        source = partner_at(k)

        @pl.when(k > 0)
        def _():
            x_copy(source, source).wait_recv()

        @pl.when(k == 0)
        def _():
            own_x.wait()

        x_norm[rows(source, half), :] = normalize(x_got[rows(source, half), :])
        return c

    def project0(i, c):
        lax.fori_loop(i * (n // 2), (i + 1) * (n // 2), norm_rows, 0)

        @pl.when((i == 0) & (s == 0))
        def _():
            wq0_local.wait()

        @pl.when((i == 0) & (s == 1))
        def _():
            wq0_remote.wait_recv()

        part = rows(lax.rem(me // (n // 2) + i, 2), tokens // 2)
        qkv0[part, :] = dot(x_norm[part, :], wq0[...]).astype(jnp.bfloat16)
        return c

    lax.fori_loop(0, 2, project0, 0)

    for h in range(HEADS):
        q = qkv0[:, h * HDIM : (h + 1) * HDIM]
        k = qkv0[:, INNER + h * HDIM : INNER + (h + 1) * HDIM]
        v = qkv0[:, 2 * INNER + h * HDIM : 2 * INNER + (h + 1) * HDIM]
        e = jnp.exp2(dot_t(q, k) * SCALE_LOG2 + bias0[...])
        w = (e * (1.0 / jnp.sum(e, axis=-1, keepdims=True))).astype(jnp.bfloat16)
        mix0[:, h * HDIM : (h + 1) * HDIM] = dot(w, v).astype(jnp.bfloat16)

    def m_copy(f, source):
        return pltpu.make_async_remote_copy(
            src_ref=mix0.at[rows(f, half), :],
            dst_ref=mix_frame.at[rows(s * n + source, half), :],
            send_sem=m_send.at[f],
            recv_sem=m_recv.at[source],
            device_id=peer(f),
            device_id_type=MESH,
        )

    per_block = BLOCK // group
    gathered = per_block * half

    def f_copy(b, core):
        place = rows(core * blocks + b, gathered)
        return pltpu.make_async_remote_copy(
            src_ref=mix_frame.at[place, :],
            dst_ref=mix_frame.at[place, :],
            send_sem=f_send.at[b],
            recv_sem=f_recv.at[b],
            device_id=sibling,
            device_id_type=MESH,
        )

    def send_m(k, c):
        m_copy(partner_at(n - k), me).start()
        return c

    lax.fori_loop(1, n, send_m, 0)
    mix_frame[rows(s * n + me, half), :] = mix0[rows(me, half), :]

    @pl.when(s == 0)
    def _():
        wo0_local.wait()

    @pl.when(s == 1)
    def _():
        wo0_remote.wait_recv()

    added = x_got[...].astype(jnp.float32) + dot(mix0[...], wo0[...])
    added = added.astype(jnp.bfloat16).reshape(n, half, -1)
    out_remote = pltpu.make_async_remote_copy(
        first0, out_ref.at[:, 1], out_send, out_recv, device_id=sibling, device_id_type=MESH
    )

    @pl.when(s == 0)
    def _():
        out_ref[:, 0] = added

    @pl.when(s == 1)
    def _():
        first0[...] = added

    frame_copy.wait()
    for j in range(3):

        @pl.when(s == 0)
        def _():
            wq1_remote[j].wait_recv()

        @pl.when(s == 1)
        def _():
            wq1_local[j].wait()

    def middle(i, c):
        def arrive(k, c):
            source = partner_at(k)
            m_copy(source, source).wait_recv()
            return c

        lax.fori_loop(jnp.maximum(i * per_block, 1), (i + 1) * per_block, arrive, 0)
        b = partner_at(i * per_block) // per_block
        f_copy(b, s).start()
        f_copy(b, 1 - s).wait_recv()
        part = rows(b, BLOCK)
        halves = [
            mix_frame[rows(core * blocks + b, gathered), :].reshape(per_block, 1, half, INNER)
            for core in range(2)
        ]
        mixed = jnp.concatenate(halves, axis=1).reshape(BLOCK, INNER)
        grown = x_frame[part, :].astype(jnp.float32) + dot(mixed, wo0[...])
        grown = grown.astype(jnp.bfloat16)
        first1[part, :] = grown
        qkv1[part, :] = dot(normalize(grown), wq1[...]).astype(jnp.bfloat16)
        return c

    lax.fori_loop(0, blocks, middle, 0)

    @pl.when(s == 1)
    def _():
        out_remote.start()

    span = tracks // 2

    def low_copy(i):
        place = pl.ds(i * span, span)
        return pltpu.make_async_remote_copy(
            src_ref=mix1.at[place, :],
            dst_ref=mix1_low.at[place, :],
            send_sem=low_send.at[i],
            recv_sem=low_recv.at[i],
            device_id=sibling,
            device_id_type=MESH,
        )

    for i in range(2):
        part = slice(i * span, (i + 1) * span)
        for h in range(HALF_HEADS):
            q = qkv1[part, h * HDIM : (h + 1) * HDIM]
            k = qkv1[:, HALF_INNER + h * HDIM : HALF_INNER + (h + 1) * HDIM]
            v = qkv1[:, 2 * HALF_INNER + h * HDIM : 2 * HALF_INNER + (h + 1) * HDIM]
            e = jnp.exp2(dot_t(q, k) * SCALE_LOG2 + bias1[part, :])
            w = (e * (1.0 / jnp.sum(e, axis=-1, keepdims=True))).astype(jnp.bfloat16)
            mix1[part, h * HDIM : (h + 1) * HDIM] = dot(w, v).astype(jnp.bfloat16)

        @pl.when(s == 0)
        def _():
            low_copy(i).start()

    @pl.when(s == 1)
    def _():
        wo1_local.wait()
        for i in range(2):
            part = slice(i * span, (i + 1) * span)
            low_copy(i).wait_recv()
            mixed = jnp.concatenate([mix1_low[part, :], mix1[part, :]], axis=1)
            total = first1[part, :].astype(jnp.float32) + dot(mixed, wo1[...])
            out_ref[i * n // 2 : (i + 1) * n // 2] = total.astype(jnp.bfloat16).reshape(
                n // 2, 2, half, -1
            )
        out_remote.wait_send()
        for copy in wq1_remote:
            copy.wait_send()

    @pl.when(s == 0)
    def _():
        out_remote.wait_recv()
        wq0_remote.wait_send()
        wo0_remote.wait_send()

        for i in range(2):
            low_copy(i).wait_send()

    def drain(k, c):
        d = partner_at(k)
        x_copy(d, me).wait_send()
        m_copy(d, me).wait_send()
        return c

    lax.fori_loop(1, n, drain, 0)

    def drain_forwards(b, c):
        f_copy(b, s).wait_send()
        return c

    lax.fori_loop(0, blocks, drain_forwards, 0)


def on_device_fused(tracks_in, w_qkv, w_out, visible, neighbours):
    n = lax.axis_size("seq")
    tracks, width = tracks_in.shape[2:]
    half = tracks // n // 2
    tokens = n * half
    blocks = tracks // BLOCK
    bf16 = jnp.bfloat16
    dma = pltpu.SemaphoreType.DMA
    in_hbm = pl.BlockSpec(memory_space=pltpu.HBM)
    out = pl.pallas_call(
        functools.partial(fused_kernel, n, half),
        out_shape=jax.ShapeDtypeStruct((n, 2, half, width), bf16),
        in_specs=[in_hbm] * 3
        + [pl.BlockSpec(memory_space=pltpu.VMEM)] * 2,
        out_specs=pl.BlockSpec(memory_space=pltpu.VMEM),
        scratch_shapes=[
            pltpu.VMEM((width, 3 * INNER), bf16),
            pltpu.VMEM((INNER, width), bf16),
            pltpu.VMEM((width, 3 * HALF_INNER), bf16),
            pltpu.VMEM((INNER, width), bf16),
            pltpu.VMEM((tokens, width), bf16),
            pltpu.VMEM((tokens, width), bf16),
            pltpu.VMEM((tracks, width), bf16),
            pltpu.VMEM((tokens, 3 * INNER), bf16),
            pltpu.VMEM((tokens, INNER), bf16),
            pltpu.VMEM((n, half, width), bf16),
            pltpu.VMEM((tracks, INNER), bf16),
            pltpu.VMEM((tracks, width), bf16),
            pltpu.VMEM((tracks, 3 * HALF_INNER), bf16),
            pltpu.VMEM((tracks, HALF_INNER), bf16),
            pltpu.VMEM((tracks, HALF_INNER), bf16),
            pltpu.VMEM((tokens, tokens), jnp.float32),
            pltpu.VMEM((tracks, tracks), jnp.float32),
            dma((6,)),
            dma((5,)),
            dma((n,)),
            dma((n,)),
            dma,
            dma((n,)),
            dma((n,)),
            dma((blocks,)),
            dma((blocks,)),
            dma((blocks,)),
            dma((blocks,)),
            dma,
            dma,
        ],
        compiler_params=pltpu.CompilerParams(
            collective_id=0, has_side_effects=True, vmem_limit_bytes=52 * 1024 * 1024
        ),
        cost_estimate=pl.CostEstimate(
            flops=9_000_000_000, bytes_accessed=20_000_000, transcendentals=1_200_000
        ),
    )(
        tracks_in.reshape(tracks, width),
        w_qkv.reshape(width, 3 * INNER),
        w_out.reshape(INNER, width),
        visible.reshape(1, tracks),
        neighbours.reshape(blocks, NB).T,
    )
    return out.reshape(1, 1, 1, tracks, width)


def fits_fused(mesh):
    return mesh.shape["seq"] == FRAMES and mesh.shape["segment"] == 2


def solution(mesh):
    body = on_device_fused if fits_fused(mesh) else on_device
    return jax.shard_map(
        body,
        mesh=mesh,
        in_specs=(
            P(None, "seq", None, None),
            P("segment", None, None),
            P("segment", None, None),
            P(None, "seq", None),
            P(),
        ),
        out_specs=P("segment", None, "seq", None, None),
        check_vma=False,
    )
```
